256 devices in a mesh: dp: 8 (over y, z_hi), tm: 32 (over z_lo, x, core).
Axes of the slice: x: 4, y: 4, z: 8 (z_hi: 2, z_lo: 4; z = z_hi * 4 + z_lo), core: 2. Of those that a mesh axis runs over, the one named last changes fastest.
Arguments:
- queries: bfloat16 [8, 4096, 1024], P('dp', 'tm'), may hold values from -6 to 6
- key_vectors: bfloat16 [8, 4096, 1024], P('dp', 'tm'), may hold values from -6 to 6
- values: bfloat16 [8, 4096, 1024], P('dp', 'tm'), may hold values from -6 to 6
- cotangent: bfloat16 [8, 4096, 2048], P('dp', 'tm'), may hold values from -6 to 6
- out_weight: bfloat16 [1024, 2048], P('tm', 'dp'), may hold values from -0.1875 to 0.1875
- offsets: int32 [8, 12], P('dp'), may hold values from 0 to 4095, as said below
Outputs:
- encoded: bfloat16 [8, 4096, 2048], P('dp', 'tm')
- grad_queries: bfloat16 [8, 4096, 1024], P('dp', 'tm')
- grad_keys: bfloat16 [8, 4096, 1024], P('dp', 'tm')
- grad_values: bfloat16 [8, 4096, 1024], P('dp', 'tm')
- grad_weight: float32 [1024, 2048], P('tm', 'dp')
The draws below stay inside these ranges and needn't reach their ends.
Inputs may be any that keep to these rules, and one draw needn't show every extreme that they name: Each row holds 12 strictly increasing frame offsets, the first of them 0 and the last 4095, so that the last utterance is the recording's final frame alone; an utterance covers the frames from its offset up to the next offset, the last one up to 4096.
All inputs are finite; a program needn't handle non-finite values.
Results may differ from the reference program's by a relative error of at most 0.0052.
Values may be sent and summed in bfloat16 or wider, within the bound.
No kernel may reach another device: no remote copies, remote signals or barrier semaphores. Data moves between devices by JAX's collectives and lax.ppermute only.
A program may use at most 192 MiB of HBM per device.

```python
import math
import jax
import jax.numpy as jnp
from jax import lax

D = 2048
HD = 128
FR_DEV = 128
UTTS = 12
HK = 1024
LEN = 4096
RECS = 8


def draw_offsets(key, part):
    key = jax.random.fold_in(key, 11)
    record_keys = jax.random.split(key, RECS)

    def one_record(record_key):
        chosen = jax.random.permutation(record_key, LEN - 2)[:UTTS - 2] + 1
        return jnp.concatenate([jnp.zeros((1,), jnp.int32), jnp.sort(chosen).astype(jnp.int32), jnp.full((1,), LEN - 1, jnp.int32)])
    return jax.vmap(one_record)(record_keys)


def block_levels(stream_key, dims, pieces, low, top_value):
    gain, own = 1.0, jax.random.fold_in(stream_key, 6)
    for position, blocks in pieces:
        heights = jnp.exp(jax.random.uniform(jax.random.fold_in(own, position), (blocks,), jnp.float32, low / len(pieces), top_value / len(pieces)))
        gain = gain * jnp.repeat(heights, dims[position] // blocks).reshape([-1 if axis == position else 1 for axis in range(len(dims))])
    return gain


def noise(rng, shape, deviation, bound, shards=(), held_as=jnp.bfloat16):
    drawn = jax.random.normal(rng, shape, jnp.float32) * deviation
    if len(shards) > 0:
        drawn = block_levels(rng, shape, shards, -0.22, 0.18) * drawn
    return jnp.clip(drawn, min=-bound, max=bound).astype(held_as)


def setup_inputs(seed: int = 0) -> dict:
    key_of = jax.random.split(jax.random.key(seed), 7)
    return {
        "queries": noise(key_of[0], (RECS, LEN, HK), 1.0, 6.0, ((0, 8), (1, 32))),
        "key_vectors": noise(key_of[1], (RECS, LEN, HK), 1.0, 6.0, ((0, 8), (1, 32))),
        "values": noise(key_of[2], (RECS, LEN, HK), 1.0, 6.0, ((0, 8), (1, 32))),
        "cotangent": noise(key_of[3], (RECS, LEN, D), 1.0, 6.0, ((0, 8), (1, 32))),
        "out_weight": noise(key_of[4], (HK, D), HK ** -0.5, 0.1875, ((0, 32), (1, 8))),
        "offsets": draw_offsets(jax.random.fold_in(key_of[6], 71), 0),
    }


def combine_open(earlier, following):
    keeping = 1.0 - following[-1]
    merged = tuple((late_state + keeping * early_state for early_state, late_state in zip(earlier[:-1], following[:-1])))
    return merged + (jnp.maximum(earlier[-1], following[-1]),)

def exclusive_forward(element):
    inclusive = lax.associative_scan(combine_open, element)
    return tuple((jnp.concatenate([jnp.zeros_like(member[:1]), member[:-1]], axis=0) for member in inclusive))

def exclusive_reverse(element):
    flipped = tuple((member[::-1] for member in element))
    result = exclusive_forward(flipped)
    return tuple((member[::-1] for member in result))

def round_half(array):
    return lax.optimization_barrier(array.astype(jnp.bfloat16)).astype(jnp.float32)

def reference(queries, key_vectors, values, cotangent, out_weight, offsets):
    head_count = queries.shape[2] // HD
    blocks = LEN // FR_DEV
    exact = lax.Precision.HIGHEST

    def per_record(inputs):
        query_rec, key_rec, value_rec, cot_rec, starts_row = inputs
        positions = jnp.arange(LEN, dtype=jnp.int32)
        utterance = lax.optimization_barrier(jnp.sum((positions[:, None] >= starts_row[None, :]).astype(jnp.int32), axis=1)) - 1
        ends_row = jnp.concatenate([starts_row[1:], jnp.full((1,), LEN, jnp.int32)])
        span_table = ends_row - starts_row
        picked = utterance[:, None] == jnp.arange(UTTS, dtype=jnp.int32)[None, :]
        span_frame = lax.optimization_barrier(jnp.sum(jnp.where(picked, span_table[None, :], 0), axis=1))
        frame_scale = 1.0 / jnp.sqrt((HD * span_frame).astype(jnp.float32))
        is_start = lax.optimization_barrier(jnp.sum((positions[:, None] == starts_row[None, :]).astype(jnp.float32), axis=1))
        back_rows = jnp.dot(cot_rec, out_weight.T, preferred_element_type=jnp.float32)
        scaled_cot = (back_rows * frame_scale[:, None]).astype(jnp.bfloat16)
        utt_blocks = utterance.reshape(blocks, FR_DEV)
        start_blocks = is_start.reshape(blocks, FR_DEV)
        scale_blocks = frame_scale.reshape(blocks, FR_DEV)
        first_mask = (utt_blocks == utt_blocks[:, :1]).astype(jnp.float32) * (1.0 - start_blocks[:, :1])
        last_mask = (utt_blocks == utt_blocks[:, -1:]).astype(jnp.float32)
        flags = jnp.minimum(lax.optimization_barrier(jnp.sum(start_blocks, axis=1)), 1.0).reshape(blocks, 1, 1, 1)
        query_f32 = query_rec.astype(jnp.float32).reshape(blocks, FR_DEV, head_count, HD)
        key_f32 = key_rec.astype(jnp.float32).reshape(blocks, FR_DEV, head_count, HD)
        value_f32 = value_rec.astype(jnp.float32).reshape(blocks, FR_DEV, head_count, HD)
        cot_f32 = scaled_cot.astype(jnp.float32).reshape(blocks, FR_DEV, head_count, HD)
        first_state = jnp.einsum('nj,njhd,njhe->nhde', first_mask, key_f32, value_f32, precision=exact)
        last_state = jnp.einsum('nj,njhd,njhe->nhde', last_mask, key_f32, value_f32, precision=exact)
        first_dstate = jnp.einsum('nj,njhd,njhe->nhde', first_mask, query_f32, cot_f32, precision=exact)
        last_dstate = jnp.einsum('nj,njhd,njhe->nhde', last_mask, query_f32, cot_f32, precision=exact)
        left_state, left_grad, unused_left = exclusive_forward((last_state, last_dstate, flags))
        right_state, right_grad, unused_right = exclusive_reverse((first_state, first_dstate, flags))

        def per_block(block_parts):
            query_blk, key_blk, value_blk, cot_blk, utt_blk, first_blk, last_blk, scale_blk, left_blk, right_blk, left_grad_blk, right_grad_blk = block_parts
            same_mask = (utt_blk[:, None] == utt_blk[None, :]).astype(jnp.float32)
            first_col = first_blk[:, None, None]
            last_col = last_blk[:, None, None]
            scores = round_half(jnp.einsum('ihd,jhd->hij', query_blk, key_blk, precision=exact) * same_mask[None])
            mixed_out = jnp.einsum('hij,jhe->ihe', scores, value_blk, precision=exact)
            mixed_out = mixed_out + first_col * jnp.einsum('ihd,hde->ihe', query_blk, left_blk, precision=exact)
            mixed_out = mixed_out + last_col * jnp.einsum('ihd,hde->ihe', query_blk, right_blk, precision=exact)
            attended_blk = (mixed_out * scale_blk[:, None, None]).astype(jnp.bfloat16)
            grad_scores = round_half(jnp.einsum('ihe,jhe->hij', cot_blk, value_blk, precision=exact) * same_mask[None])
            grad_query = jnp.einsum('hij,jhd->ihd', grad_scores, key_blk, precision=exact)
            grad_query = grad_query + first_col * jnp.einsum('ihe,hde->ihd', cot_blk, left_blk, precision=exact)
            grad_query = grad_query + last_col * jnp.einsum('ihe,hde->ihd', cot_blk, right_blk, precision=exact)
            grad_key = jnp.einsum('hij,ihd->jhd', grad_scores, query_blk, precision=exact)
            grad_key = grad_key + first_col * jnp.einsum('jhe,hde->jhd', value_blk, left_grad_blk, precision=exact)
            grad_key = grad_key + last_col * jnp.einsum('jhe,hde->jhd', value_blk, right_grad_blk, precision=exact)
            grad_value = jnp.einsum('hij,ihe->jhe', scores, cot_blk, precision=exact)
            grad_value = grad_value + first_col * jnp.einsum('jhd,hde->jhe', key_blk, left_grad_blk, precision=exact)
            grad_value = grad_value + last_col * jnp.einsum('jhd,hde->jhe', key_blk, right_grad_blk, precision=exact)
            return (attended_blk, grad_query.astype(jnp.bfloat16), grad_key.astype(jnp.bfloat16), grad_value.astype(jnp.bfloat16))
        attended, grad_query, grad_key, grad_value = lax.map(per_block, (query_f32, key_f32, value_f32, cot_f32, utt_blocks, first_mask, last_mask, scale_blocks, left_state, right_state, left_grad, right_grad))
        attended = attended.reshape(LEN, HK)
        encoded = jnp.dot(attended, out_weight, preferred_element_type=jnp.float32).astype(jnp.bfloat16)
        weight_term = jnp.dot(attended.T, cot_rec, preferred_element_type=jnp.float32)
        return (encoded, grad_query.reshape(LEN, HK), grad_key.reshape(LEN, HK), grad_value.reshape(LEN, HK), weight_term)
    encoded, grad_queries, grad_keys, grad_values, weight_terms = lax.map(per_record, (queries, key_vectors, values, cotangent, offsets))
    grad_weight = lax.optimization_barrier(jnp.sum(weight_terms, axis=0)) / math.sqrt(RECS * LEN)
    return (encoded, grad_queries, grad_keys, grad_values, grad_weight)
```

```python
import math

import jax
import jax.numpy as jnp
import numpy as np
from jax import lax
from jax.sharding import Mesh
from jax.sharding import PartitionSpec as P

HD = 128
Y, H, Z, X, C = 4, 2, 4, 4, 2
PLANE = ("x", "c")
ACROSS = ("y", "h", "z")
ALL = ("y", "h", "z", "x", "c")
BF = jnp.bfloat16
F32 = jnp.float32


def flat(y, h, z, x, c):
    return (((y * H + h) * Z + z) * X + x) * C + c


def swap_pairs():
    return [
        (flat(y, h, z, x, c), flat(y, c, x, z, h))
        for y in range(Y)
        for h in range(H)
        for z in range(Z)
        for x in range(X)
        for c in range(C)
    ]


def mm(a, b, dims):
    return lax.dot_general(a, b, (dims, ((), ())), preferred_element_type=F32)


def body(queries, key_vectors, values, cotangent, out_weight, offsets):
    plane = lax.axis_index("z")
    core = lax.axis_index("c")
    frames = queries.shape[1]
    chunk = frames * X * C
    length = chunk * Z
    starts = offsets[0]
    utts = starts.shape[0]

    positions = plane * chunk + jnp.arange(chunk, dtype=jnp.int32)
    utterance = jnp.sum((positions[:, None] >= starts[None, :]).astype(jnp.int32), axis=1) - 1
    ends = jnp.concatenate([starts[1:], jnp.full((1,), length, jnp.int32)])
    picked = utterance[:, None] == jnp.arange(utts, dtype=jnp.int32)[None, :]
    span = jnp.sum(jnp.where(picked, (ends - starts)[None, :], 0), axis=1)
    scale = (1.0 / jnp.sqrt((HD * span).astype(F32)))[:, None]
    mask = picked.astype(BF)
    plane_first = jnp.arange(Z, dtype=jnp.int32) * chunk
    first_utt = jnp.sum((plane_first[:, None] >= starts[None, :]).astype(jnp.int32), axis=1) - 1
    last_utt = (
        jnp.sum((plane_first[:, None] + (chunk - 1) >= starts[None, :]).astype(jnp.int32), axis=1)
        - 1
    )
    slots = jnp.arange(utts, dtype=jnp.int32)
    other = (jnp.arange(Z) != plane)[:, None]
    take_first = ((slots[None, :] == first_utt[:, None]) & other).astype(F32)
    take_last = (
        (slots[None, :] == last_utt[:, None]) & other & (last_utt != first_utt)[:, None]
    ).astype(F32)

    def spread(rows):
        return (rows[:, None, :] * mask[:, :, None]).reshape(chunk, utts * HD)

    def totals(left, right):
        own = mm(spread(left), right, ((0,), (0,))).reshape(utts, HD, HD)
        first = lax.dynamic_index_in_dim(own, first_utt[plane], 0, False)
        last = lax.dynamic_index_in_dim(own, last_utt[plane], 0, False)
        edge = jnp.stack([first, last])
        edges = lax.all_to_all(jnp.broadcast_to(edge[None], (Z, 2, HD, HD)), "z", 0, 0, tiled=True)
        for z in range(Z):
            own = own + take_first[z][:, None, None] * edges[z, 0]
            own = own + take_last[z][:, None, None] * edges[z, 1]
        return own.astype(BF)

    heads = jnp.stack(
        [
            part[0].reshape(frames, X * C, HD).transpose(1, 0, 2)
            for part in (queries, key_vectors, values)
        ],
        axis=1,
    )
    heads = lax.all_to_all(heads, PLANE, 0, 0, tiled=True)
    query, key, value = (heads[:, i].reshape(chunk, HD) for i in range(3))

    moved = lax.ppermute(out_weight, ALL, swap_pairs())
    group = Y * H * Z
    pieces = lax.all_to_all(
        jnp.broadcast_to(moved[None], (group,) + moved.shape), ACROSS, 0, 0, tiled=True
    )
    rows, cols = moved.shape
    block = (
        pieces.reshape(Y, H, Z, rows, cols).transpose(2, 1, 3, 0, 4).reshape(2 * HD, Y * cols)
    )
    weight = lax.all_gather(block, PLANE, axis=0)

    cot_half = cotangent[0].reshape(frames, Y, C, cols).transpose(2, 0, 1, 3)
    cot_half = cot_half.reshape(1, C, frames, Y * cols)
    cot = lax.all_to_all(
        jnp.broadcast_to(cot_half, (X, C, frames, Y * cols)).reshape(X * C, frames, Y * cols),
        PLANE,
        0,
        0,
        tiled=True,
    ).reshape(chunk, Y * cols)

    state = totals(key, value).reshape(utts * HD, HD)
    attended = (mm(spread(query), state, ((1,), (0,))) * scale).astype(BF)

    back = mm(cot, block, ((1,), (1,)))
    swap = [(0, 1), (1, 0)]
    mine = lax.dynamic_slice_in_dim(back, core * HD, HD, 1)
    theirs = lax.dynamic_slice_in_dim(back, (1 - core) * HD, HD, 1)
    scaled_cot = ((mine + lax.ppermute(theirs, "c", swap)) * scale).astype(BF)

    partner = lax.ppermute(attended, "c", swap)
    low = jnp.where(core == 0, attended, partner)
    high = jnp.where(core == 0, partner, attended)
    pair = jnp.concatenate([low, high], axis=1)
    term = mm(pair, cot, ((0,), (0,))).astype(BF)
    term = term.reshape(Z, H, rows, Y, cols).transpose(3, 1, 0, 2, 4).reshape(group, rows, cols)
    term = lax.all_to_all(term, ACROSS, 0, 0, tiled=True)
    grad_weight = jnp.sum(term.astype(F32), axis=0) / math.sqrt(Y * H * length)
    grad_weight = lax.ppermute(grad_weight, ALL, swap_pairs())

    grad = totals(query, scaled_cot)
    spread_key = spread(key)
    grad_value = mm(spread_key, grad.reshape(utts * HD, HD), ((1,), (0,))).astype(BF)
    grad_t = grad.transpose(0, 2, 1).reshape(utts * HD, HD)
    grad_key = mm(spread(value), grad_t, ((1,), (0,))).astype(BF)
    state_t = state.reshape(utts, HD, HD).transpose(0, 2, 1).reshape(utts * HD, HD)
    grad_query = mm(spread(scaled_cot), state_t, ((1,), (0,))).astype(BF)

    def home(parts):
        stacked = jnp.stack([part.reshape(X * C, frames, HD) for part in parts], axis=1)
        got = lax.all_to_all(stacked, PLANE, 0, 0, tiled=True)
        return [
            got[:, i].transpose(1, 0, 2).reshape(frames, X * C * HD) for i in range(len(parts))
        ]

    (attended_rows,) = home([attended])
    wide = weight.reshape(X, C, 2 * HD, Y, cols)
    encoded = jnp.stack(
        [mm(attended_rows, wide[:, c].reshape(X * 2 * HD, Y * cols), ((1,), (0,))) for c in range(C)]
    ).astype(BF)
    encoded = encoded.reshape(C, frames, Y, cols).transpose(1, 2, 0, 3).reshape(frames, Y * C * cols)
    grads = home([grad_query, grad_key, grad_value])
    return (encoded[None], grads[0][None], grads[1][None], grads[2][None], grad_weight)


def solution(mesh):
    fine = Mesh(np.asarray(mesh.devices).reshape(Y, H, Z, X, C), ALL)
    dp, tm = ("y", "h"), ("z", "x", "c")
    three = P(dp, tm, None)
    in_specs = (three, three, three, three, P(tm, dp), P(dp, None))
    out_specs = (three, three, three, three, P(tm, dp))
    return jax.shard_map(body, mesh=fine, in_specs=in_specs, out_specs=out_specs, check_vma=False)
```

```python
import math

import jax
import jax.numpy as jnp
import numpy as np
from jax import lax
from jax.experimental import pallas as pl
from jax.experimental.pallas import tpu as pltpu
from jax.sharding import Mesh
from jax.sharding import PartitionSpec as P

HD = 128
FRAMES = 128
Y, H, Z, X, C = 4, 2, 4, 4, 2
BLOCKS = X * C
CHUNK = BLOCKS * FRAMES
LENGTH = Z * CHUNK
UTTS = 12
ROWS = 32
COLS = 256
HALF = Y * COLS
ALL = ("y", "h", "z", "x", "c")
PLANE = ("x", "c")
ACROSS = ("y", "h", "z")
BF = jnp.bfloat16
F32 = jnp.float32

VMEM = pl.BlockSpec(memory_space=pltpu.VMEM)
SMEM = pl.BlockSpec(memory_space=pltpu.SMEM)


def call(kernel, outs, *args, scratch=(), smem=0):
    return pl.pallas_call(
        kernel,
        out_shape=[jax.ShapeDtypeStruct(shape, dtype) for shape, dtype in outs],
        in_specs=[SMEM] * smem + [VMEM] * (len(args) - smem),
        out_specs=[VMEM] * len(outs),
        scratch_shapes=list(scratch),
        compiler_params=pltpu.CompilerParams(vmem_limit_bytes=40 * 1024 * 1024),
    )(*args)


def dot(a, b, left=1, right=0):
    return lax.dot_general(
        a, b, (((left,), (right,)), ((), ())), preferred_element_type=F32
    )


def limits(off_ref, u, plane):
    base = plane * CHUNK
    end = off_ref[0, u + 1] if u + 1 < UTTS else LENGTH
    return off_ref[0, u] - base, end - base


def present(off_ref, u, plane):
    low, high = limits(off_ref, u, plane)
    return (low < CHUNK) & (high > 0)


def row_mask(off_ref, u, plane):
    low, high = limits(off_ref, u, plane)
    rows = lax.broadcasted_iota(jnp.int32, (CHUNK, HD), 0)
    return (rows >= low) & (rows < high)


def lane_mask(off_ref, u, plane):
    low, high = limits(off_ref, u, plane)
    lanes = lax.broadcasted_iota(jnp.int32, (HD, CHUNK), 1)
    return (lanes >= low) & (lanes < high)


def scale_of(off_ref, u, plane):
    low, high = limits(off_ref, u, plane)
    span = jnp.full((1, HD), HD * (high - low), jnp.int32).astype(F32)
    return 1.0 / jnp.sqrt(span)


def utterance_at(off_ref, frame):
    count = jnp.int32(-1)
    for u in range(UTTS):
        count = count + (off_ref[0, u] <= frame).astype(jnp.int32)
    return count


def partial_sums(off_ref, plane, left_t, right, own_ref, edge_ref):
    for u in range(UTTS):

        @pl.when(present(off_ref, u, plane))
        def _(u=u):
            masked = jnp.where(lane_mask(off_ref, u, plane), left_t, 0.0).astype(BF)
            own_ref[u] = dot(masked, right)

    first = utterance_at(off_ref, plane * CHUNK)
    last = utterance_at(off_ref, plane * CHUNK + CHUNK - 1)
    edge_ref[0] = own_ref[first]
    edge_ref[1] = own_ref[last]


def edge_utterances(off_ref, plane):
    found = []
    for shift in range(1, Z):
        source = lax.rem(plane + Z - shift, Z)
        first = utterance_at(off_ref, source * CHUNK)
        last = utterance_at(off_ref, source * CHUNK + CHUNK - 1)
        found.append((first, jnp.where(last == first, -1, last)))
    return found


def whole_sum(u, own_ref, edge_refs, found):
    total = own_ref[u]
    for edge_ref, (first, last) in zip(edge_refs, found):
        total = total + edge_ref[0] * (first == u).astype(F32)
        total = total + edge_ref[1] * (last == u).astype(F32)
    return total.astype(BF)


def prepare_kernel(q_ref, k_ref, v_ref, cot_ref, heads_ref, keep_ref, give_ref):
    core = lax.axis_index("c")
    for head in range(BLOCKS):
        columns = slice(head * HD, (head + 1) * HD)
        heads_ref[head, 0] = q_ref[0, :, columns]
        heads_ref[head, 1] = k_ref[0, :, columns]
        heads_ref[head, 2] = v_ref[0, :, columns]

    def halves(zero_ref, one_ref):
        for y in range(Y):
            start = y * C * COLS
            zero_ref[:, y * COLS : (y + 1) * COLS] = cot_ref[0, :, start : start + COLS]
            one_ref[:, y * COLS : (y + 1) * COLS] = cot_ref[0, :, start + COLS : start + 2 * COLS]

    @pl.when(core == 0)
    def _():
        halves(keep_ref, give_ref)

    @pl.when(core == 1)
    def _():
        halves(give_ref, keep_ref)


def state_kernel(off_ref, heads_ref, own_ref, edge_ref):
    plane = lax.axis_index("z")
    key = heads_ref[:, 1].reshape(CHUNK, HD).astype(F32)
    value = heads_ref[:, 2].reshape(CHUNK, HD)
    partial_sums(off_ref, plane, key.T, value, own_ref, edge_ref)


def attended_kernel(off_ref, heads_ref, own_ref, e1, e2, e3, attended_ref, state_ref, total_ref):
    plane = lax.axis_index("z")
    found = edge_utterances(off_ref, plane)
    query = heads_ref[:, 0].reshape(CHUNK, HD)
    for u in range(UTTS):

        @pl.when(present(off_ref, u, plane))
        def _(u=u):
            state = whole_sum(u, own_ref, (e1, e2, e3), found)
            state_ref[u] = state
            rows = dot(query, state) * scale_of(off_ref, u, plane)
            total_ref[...] = jnp.where(row_mask(off_ref, u, plane), rows, total_ref[...])

    attended_ref[...] = total_ref[...].astype(BF).reshape(BLOCKS, FRAMES, HD)


def block_order():
    x = lax.axis_index("x")
    c = lax.axis_index("c")
    sources = (x, lax.rem(x + X - 1, X), lax.rem(x + 1, X), lax.rem(x + 2, X))
    return [source * C + core for source in sources for core in (c, 1 - c)]


def cotangent_kernel(pieces_ref, *refs):
    cots, (mine_ref, theirs_ref, weight_ref) = refs[:BLOCKS], refs[BLOCKS:]
    core = lax.axis_index("c")
    for y in range(Y):
        for h in range(H):
            for z in range(Z):
                row = (z * H + h) * ROWS
                weight_ref[row : row + ROWS, y * COLS : (y + 1) * COLS] = pieces_ref[
                    (y * H + h) * Z + z
                ]
    weight = weight_ref[...]
    for cot_ref, block in zip(cots, block_order()):
        back = dot(cot_ref[...], weight, 1, 1)
        low, high = back[:, :HD], back[:, HD:]
        mine_ref[block] = jnp.where(core == 0, low, high)
        theirs_ref[block] = jnp.where(core == 0, high, low)


def gradient_kernel(off_ref, heads_ref, mine_ref, came_ref, scaled_ref, own_ref, edge_ref, total_ref):
    plane = lax.axis_index("z")
    back = (mine_ref[...] + came_ref[...]).reshape(CHUNK, HD)
    for u in range(UTTS):

        @pl.when(present(off_ref, u, plane))
        def _(u=u):
            rows = back * scale_of(off_ref, u, plane)
            total_ref[...] = jnp.where(row_mask(off_ref, u, plane), rows, total_ref[...])

    scaled = total_ref[...].astype(BF)
    scaled_ref[...] = scaled
    query = heads_ref[:, 0].reshape(CHUNK, HD).astype(F32)
    partial_sums(off_ref, plane, query.T, scaled, own_ref, edge_ref)


def home_kernel(off_ref, heads_ref, scaled_ref, state_ref, own_ref, e1, e2, e3, out_ref, gq, gk, gv):
    plane = lax.axis_index("z")
    found = edge_utterances(off_ref, plane)
    key = heads_ref[:, 1].reshape(CHUNK, HD)
    value = heads_ref[:, 2].reshape(CHUNK, HD)
    scaled = scaled_ref[...]
    for u in range(UTTS):

        @pl.when(present(off_ref, u, plane))
        def _(u=u):
            grad = whole_sum(u, own_ref, (e1, e2, e3), found)
            mask = row_mask(off_ref, u, plane)
            gq[...] = jnp.where(mask, dot(scaled, state_ref[u], 1, 1), gq[...])
            gk[...] = jnp.where(mask, dot(value, grad, 1, 1), gk[...])
            gv[...] = jnp.where(mask, dot(key, grad), gv[...])

    for place, ref in enumerate((gq, gk, gv)):
        out_ref[:, place] = ref[...].astype(BF).reshape(BLOCKS, FRAMES, HD)


def weight_kernel(own_ref, partner_ref, *refs):
    cots, (term_ref, s0, s1, s2, s3, pair_ref) = refs[:BLOCKS], refs[BLOCKS:]
    core = lax.axis_index("c")
    x = lax.axis_index("x")
    own, partner = own_ref[...], partner_ref[...]

    @pl.when(core == 0)
    def _():
        pair_ref[:, :, :HD] = own
        pair_ref[:, :, HD:] = partner

    @pl.when(core == 1)
    def _():
        pair_ref[:, :, :HD] = partner
        pair_ref[:, :, HD:] = own

    for shift, ref in enumerate((s0, s1, s2, s3)):
        target = lax.rem(x + shift, X) * C
        for c in range(C):
            ref[c] = pair_ref[target + c]
    order = block_order()
    term = None
    for i in range(0, BLOCKS, 2):
        left = jnp.concatenate([pair_ref[order[i]], pair_ref[order[i + 1]]], axis=0)
        right = jnp.concatenate([cots[i][...], cots[i + 1][...]], axis=0)
        part = dot(left, right, 0, 0)
        term = part if term is None else term + part
    term = term.astype(BF)
    for y in range(Y):
        for h in range(H):
            for z in range(Z):
                row = (z * H + h) * ROWS
                term_ref[(y * H + h) * Z + z] = term[
                    row : row + ROWS, y * COLS : (y + 1) * COLS
                ]


def encode_kernel(a0, a1, a2, a3, w0, w1, w2, top, bottom, mine_ref, theirs_ref):
    core = lax.axis_index("c")
    total = None
    for a_ref, w in (
        (a0, w0[...]),
        (a1, w1[...]),
        (a2, w2[...]),
        (a3, jnp.concatenate([top[...], bottom[...]], axis=0)),
    ):
        part = dot(a_ref[...].reshape(C * FRAMES, 2 * HD), w)
        total = part if total is None else total + part
    total = total.astype(BF)
    zero, one = total[:FRAMES], total[FRAMES:]

    @pl.when(core == 0)
    def _():
        mine_ref[...] = zero
        theirs_ref[...] = one

    @pl.when(core == 1)
    def _():
        mine_ref[...] = one
        theirs_ref[...] = zero


def encoded_kernel(mine_ref, came_ref, out_ref):
    core = lax.axis_index("c")

    def place(zero_ref, one_ref):
        for y in range(Y):
            start = y * C * COLS
            columns = slice(y * COLS, (y + 1) * COLS)
            out_ref[0, :, start : start + COLS] = zero_ref[:, columns]
            out_ref[0, :, start + COLS : start + 2 * COLS] = one_ref[:, columns]

    @pl.when(core == 0)
    def _():
        place(mine_ref, came_ref)

    @pl.when(core == 1)
    def _():
        place(came_ref, mine_ref)


def grads_kernel(got_ref, q_ref, k_ref, v_ref):
    for head in range(BLOCKS):
        columns = slice(head * HD, (head + 1) * HD)
        for place, ref in enumerate((q_ref, k_ref, v_ref)):
            ref[0, :, columns] = got_ref[head, place]


def flat(y, h, z, x, c):
    return (((y * H + h) * Z + z) * X + x) * C + c


def swap_pairs():
    return [
        (flat(y, h, z, x, c), flat(y, c, x, z, h))
        for y in range(Y)
        for h in range(H)
        for z in range(Z)
        for x in range(X)
        for c in range(C)
    ]


def turn(value, axis, size, shift):
    return lax.ppermute(value, axis, [(i, (i + shift) % size) for i in range(size)])


def swap_cores(value):
    return turn(value, "c", C, 1)


def edges_of(edge):
    return [turn(edge, "z", Z, shift) for shift in range(1, Z)]


def body(queries, key_vectors, values, cotangent, out_weight, offsets):
    group = Y * H * Z
    state_shape = (UTTS, HD, HD)
    edge_shape = (2, HD, HD)
    chunk_scratch = pltpu.VMEM((CHUNK, HD), F32)

    moved = lax.ppermute(out_weight, ALL, swap_pairs())
    heads, keep, give = call(
        prepare_kernel,
        [((BLOCKS, 3, FRAMES, HD), BF), ((FRAMES, HALF), BF), ((FRAMES, HALF), BF)],
        queries,
        key_vectors,
        values,
        cotangent,
    )
    partner = swap_cores(give)
    back_keep, back_partner = turn(keep, "x", X, 1), turn(partner, "x", X, 1)
    next_keep, next_partner = turn(keep, "x", X, -1), turn(partner, "x", X, -1)
    far_keep, far_partner = turn(back_keep, "x", X, 1), turn(next_partner, "x", X, -1)
    cots = [keep, partner, back_keep, back_partner, next_keep, next_partner, far_keep, far_partner]

    heads = lax.all_to_all(heads, PLANE, 0, 0, tiled=True)
    pieces = lax.all_to_all(
        jnp.broadcast_to(moved[None], (group, ROWS, COLS)), ACROSS, 0, 0, tiled=True
    )

    own, edge = call(
        state_kernel, [(state_shape, F32), (edge_shape, F32)], offsets, heads, smem=1
    )
    attended, state = call(
        attended_kernel,
        [((BLOCKS, FRAMES, HD), BF), (state_shape, BF)],
        offsets,
        heads,
        own,
        *edges_of(edge),
        scratch=[chunk_scratch],
        smem=1,
    )
    term, s0, s1, s2, s3 = call(
        weight_kernel,
        [((group, ROWS, COLS), BF)] + [((C, FRAMES, 2 * HD), BF)] * X,
        attended,
        swap_cores(attended),
        *cots,
        scratch=[pltpu.VMEM((BLOCKS, FRAMES, 2 * HD), BF)],
    )
    a1, a2, a3 = turn(s1, "x", X, 1), turn(s3, "x", X, -1), turn(s2, "x", X, 2)

    mine, theirs, weight = call(
        cotangent_kernel,
        [((BLOCKS, FRAMES, HD), F32)] * 2 + [((2 * HD, HALF), BF)],
        pieces,
        *cots,
    )
    scaled, gown, gedge = call(
        gradient_kernel,
        [((CHUNK, HD), BF), (state_shape, F32), (edge_shape, F32)],
        offsets,
        heads,
        mine,
        swap_cores(theirs),
        scratch=[chunk_scratch],
        smem=1,
    )
    w1, w2 = turn(weight, "x", X, 1), turn(weight, "x", X, -1)
    top, bottom = turn(w1[:HD], "x", X, 1), turn(w2[HD:], "x", X, -1)

    term = lax.all_to_all(term, ACROSS, 0, 0, tiled=True)
    grad_weight = jnp.sum(term.astype(F32), axis=0) / math.sqrt(Y * H * LENGTH)
    grad_weight = lax.ppermute(grad_weight, ALL, swap_pairs())

    (homeward,) = call(
        home_kernel,
        [((BLOCKS, 3, FRAMES, HD), BF)],
        offsets,
        heads,
        scaled,
        state,
        gown,
        *edges_of(gedge),
        scratch=[chunk_scratch] * 3,
        smem=1,
    )
    mine, theirs = call(
        encode_kernel,
        [((FRAMES, HALF), BF)] * 2,
        s0,
        a1,
        a2,
        a3,
        weight,
        w1,
        w2,
        top,
        bottom,
    )
    (encoded,) = call(
        encoded_kernel, [((1, FRAMES, C * HALF), BF)], mine, swap_cores(theirs)
    )
    got = lax.all_to_all(homeward, PLANE, 0, 0, tiled=True)
    grads = call(grads_kernel, [((1, FRAMES, BLOCKS * HD), BF)] * 3, got)
    return (encoded, grads[0], grads[1], grads[2], grad_weight)


def solution(mesh):
    fine = Mesh(np.asarray(mesh.devices).reshape(Y, H, Z, X, C), ALL)
    dp, tm = ("y", "h"), ("z", "x", "c")
    three = P(dp, tm, None)
    in_specs = (three, three, three, three, P(tm, dp), P(dp, None))
    out_specs = (three, three, three, three, P(tm, dp))
    return jax.shard_map(body, mesh=fine, in_specs=in_specs, out_specs=out_specs, check_vma=False)
```

```python
import math

import jax
import jax.numpy as jnp
import numpy as np
from jax import lax
from jax.experimental import pallas as pl
from jax.experimental.pallas import tpu as pltpu
from jax.sharding import Mesh
from jax.sharding import PartitionSpec as P

HD = 128
FRAMES = 128
Y, H, Z, X, C = 4, 2, 4, 4, 2
BLOCKS = X * C
CHUNK = BLOCKS * FRAMES
LENGTH = Z * CHUNK
UTTS = 12
ROWS = 32
COLS = 256
HALF = Y * COLS
TILES = HALF // HD
PASSED = TILES + 3
ALL = ("y", "h", "z", "x", "c")
ACROSS = ("y", "h", "z")
BF = jnp.bfloat16
F32 = jnp.float32

VMEM = pl.BlockSpec(memory_space=pltpu.VMEM)
SMEM = pl.BlockSpec(memory_space=pltpu.SMEM)


def call(kernel, outs, *args, scratch=(), smem=0, where=pltpu.VMEM, after=(), mib=40):
    count = len(args)

    def run(*refs):
        kernel(*refs[:count], *refs[count + len(after) :])

    specs = [SMEM] * smem + [pl.BlockSpec(memory_space=where)] * (count - smem)
    return pl.pallas_call(
        run,
        out_shape=[jax.ShapeDtypeStruct(shape, dtype) for shape, dtype in outs],
        in_specs=specs + [pl.BlockSpec(memory_space=pl.ANY)] * len(after),
        out_specs=[VMEM] * len(outs),
        scratch_shapes=list(scratch),
        compiler_params=pltpu.CompilerParams(vmem_limit_bytes=mib * 1024 * 1024),
    )(*args, *after)


def dot(a, b, left=1, right=0):
    return lax.dot_general(
        a, b, (((left,), (right,)), ((), ())), preferred_element_type=F32
    )


def limits(off_ref, u, plane):
    base = plane * CHUNK
    end = off_ref[0, u + 1] if u + 1 < UTTS else LENGTH
    return off_ref[0, u] - base, end - base


def present(off_ref, u, plane):
    low, high = limits(off_ref, u, plane)
    return (low < CHUNK) & (high > 0)


def row_mask(off_ref, u, plane):
    low, high = limits(off_ref, u, plane)
    rows = lax.broadcasted_iota(jnp.int32, (CHUNK, HD), 0)
    return (rows >= low) & (rows < high)


def lane_mask(off_ref, u, plane):
    low, high = limits(off_ref, u, plane)
    lanes = lax.broadcasted_iota(jnp.int32, (HD, CHUNK), 1)
    return (lanes >= low) & (lanes < high)


def scale_of(off_ref, u, plane):
    low, high = limits(off_ref, u, plane)
    span = jnp.full((1, HD), HD * (high - low), jnp.int32).astype(F32)
    return 1.0 / jnp.sqrt(span)


def utterance_at(off_ref, frame):
    count = jnp.int32(-1)
    for u in range(UTTS):
        count = count + (off_ref[0, u] <= frame).astype(jnp.int32)
    return count


def partial_sums(off_ref, plane, left_t, right, own_ref):
    for u in range(UTTS):

        @pl.when(present(off_ref, u, plane))
        def _(u=u):
            masked = jnp.where(lane_mask(off_ref, u, plane), left_t, 0.0).astype(BF)
            own_ref[u] = dot(masked, right)

    first = utterance_at(off_ref, plane * CHUNK)
    last = utterance_at(off_ref, plane * CHUNK + CHUNK - 1)
    return [
        own_ref[jnp.where(plane + shift < Z, last, first)].astype(BF) for shift in range(1, Z)
    ]


def edge_utterances(off_ref, plane):
    found = []
    for shift in range(1, Z):
        source = lax.rem(plane + Z - shift, Z)
        frame = source * CHUNK + jnp.where(source < plane, CHUNK - 1, 0)
        found.append(utterance_at(off_ref, frame))
    return found


def whole_sum(u, own_ref, edge_refs, which, found):
    total = own_ref[u]
    for edge_ref, utterance in zip(edge_refs, found):
        total = total + edge_ref[which].astype(F32) * (utterance == u).astype(F32)
    return total.astype(BF)


def prepare_kernel(q_ref, k_ref, v_ref, cot_ref, keep_ref, give_ref, sems):
    core = lax.axis_index("c")
    copies = []
    for side, (ref, whose) in enumerate(((give_ref, 1 - core), (keep_ref, core))):
        for pair in range(X):
            start = pl.multiple_of((pair * C + whose) * HD, HD)
            for place, source in enumerate((q_ref, k_ref, v_ref)):
                copies.append((source.at[0, :, pl.ds(start, HD)], ref.at[pair * 3 + place], side))
        for tile in range(TILES):
            start = (tile // 2) * C * COLS + whose * COLS + (tile % 2) * HD
            start = pl.multiple_of(start, HD)
            copies.append((cot_ref.at[0, :, pl.ds(start, HD)], ref.at[X * 3 + tile], side))
    copies = [
        pltpu.make_async_copy(source, target, sems.at[i])
        for i, (source, target, _) in enumerate(copies)
    ]
    for copy in copies:
        copy.start()
    for copy in copies:
        copy.wait()


def merge_kernel(keep_ref, came_ref, self_ref, next_ref, back_ref):
    core = lax.axis_index("c")
    x = lax.axis_index("x")
    far = lax.rem(x + 2, X) * 3
    for mine, block in ((keep_ref, core), (came_ref, 1 - core)):
        for first, out, shift in ((0, next_ref, 1), (1, back_ref, 3)):
            near = lax.rem(x + shift, X) * 3
            cot = jnp.where(block == first, 0, PASSED)
            out[pl.ds(cot, TILES)] = mine[X * 3 :]
            out[pl.ds(PASSED + TILES + block * 3, 3)] = mine[pl.ds(near, 3)]

            @pl.when(block == first)
            def _(mine=mine, out=out):
                out[TILES:PASSED] = mine[pl.ds(far, 3)]

        self_ref[pl.ds(block * TILES, TILES)] = mine[X * 3 :]
        self_ref[pl.ds(C * TILES + block * 3, 3)] = mine[pl.ds(x * 3, 3)]


def sources():
    x = lax.axis_index("x")
    return (x, lax.rem(x + X - 1, X), lax.rem(x + 1, X), lax.rem(x + 2, X))


def state_kernel(off_ref, s0, s1, s2, far0, far1, heads_ref, own_ref, edge_ref):
    plane = lax.axis_index("z")
    parts = [[ref[start : start + 3] for start in starts] for ref, starts in (
        (s0, (C * TILES, C * TILES + 3)),
        (s1, (PASSED + TILES, PASSED + TILES + 3)),
        (s2, (PASSED + TILES, PASSED + TILES + 3)),
    )]
    parts.append([far0[TILES:], far1[TILES:]])
    for pair, source in zip(parts, sources()):
        for core, part in enumerate(pair):
            heads_ref[source * C + core] = part
    key = heads_ref[:, 1].reshape(CHUNK, HD).astype(F32)
    value = heads_ref[:, 2].reshape(CHUNK, HD)
    edges = partial_sums(off_ref, plane, key.T, value, own_ref)
    for place, edge in enumerate(edges):
        edge_ref[place] = edge


def attended_kernel(off_ref, heads_ref, own_ref, e1, e2, e3, attended_ref, state_ref, total_ref):
    plane = lax.axis_index("z")
    found = edge_utterances(off_ref, plane)
    query = heads_ref[:, 0].reshape(CHUNK, HD)
    for u in range(UTTS):

        @pl.when(present(off_ref, u, plane))
        def _(u=u):
            state = whole_sum(u, own_ref, (e1, e2, e3), 0, found)
            state_ref[u] = state
            rows = dot(query, state) * scale_of(off_ref, u, plane)
            total_ref[...] = jnp.where(row_mask(off_ref, u, plane), rows, total_ref[...])

    attended_ref[...] = total_ref[...].astype(BF).reshape(BLOCKS, FRAMES, HD)


def wide(tiles):
    return jnp.concatenate([tiles[i] for i in range(TILES)], axis=1)


def chip_cotangents(s0, s1, s2, far0, far1):
    parts = (
        (s0[:TILES], s0[TILES : 2 * TILES]),
        (s1[:TILES], s1[PASSED : PASSED + TILES]),
        (s2[PASSED : PASSED + TILES], s2[:TILES]),
        (far0[:TILES], far1[:TILES]),
    )
    for pair, source in zip(parts, sources()):
        yield source, jnp.concatenate([wide(part) for part in pair], axis=0)


def block_kernel(pieces_ref, weight_ref):
    for y in range(Y):
        for h in range(H):
            for z in range(Z):
                row = (z * H + h) * ROWS
                weight_ref[row : row + ROWS, y * COLS : (y + 1) * COLS] = pieces_ref[
                    (y * H + h) * Z + z
                ]


def cotangent_kernel(weight_ref, s0, s1, s2, far0, far1, mine_ref, theirs_ref):
    core = lax.axis_index("c")
    weight = weight_ref[...]
    for source, rows in chip_cotangents(s0, s1, s2, far0, far1):
        back = dot(rows, weight, 1, 1)
        low, high = back[:, :HD], back[:, HD:]
        mine = jnp.where(core == 0, low, high)
        theirs = jnp.where(core == 0, high, low)
        for c in range(C):
            mine_ref[source * C + c] = mine[c * FRAMES : (c + 1) * FRAMES]
            theirs_ref[source * C + c] = theirs[c * FRAMES : (c + 1) * FRAMES]


def gradient_kernel(
    off_ref, heads_ref, mine_ref, came_ref, edge_ref, scaled_ref, own_ref, o1, o2, o3, total_ref
):
    plane = lax.axis_index("z")
    back = (mine_ref[...] + came_ref[...]).reshape(CHUNK, HD)
    for u in range(UTTS):

        @pl.when(present(off_ref, u, plane))
        def _(u=u):
            rows = back * scale_of(off_ref, u, plane)
            total_ref[...] = jnp.where(row_mask(off_ref, u, plane), rows, total_ref[...])

    scaled = total_ref[...].astype(BF)
    scaled_ref[...] = scaled
    query = heads_ref[:, 0].reshape(CHUNK, HD).astype(F32)
    edges = partial_sums(off_ref, plane, query.T, scaled, own_ref)
    for place, (edge, out) in enumerate(zip(edges, (o1, o2, o3))):
        out[0] = edge_ref[place]
        out[1] = edge


def weight_kernel(own_ref, partner_ref, s0, s1, s2, far0, far1, term_ref, pair_ref):
    core = lax.axis_index("c")
    own, partner = own_ref[...], partner_ref[...]
    pair_ref[:, 0] = jnp.where(core == 0, own, partner)
    pair_ref[:, 1] = jnp.where(core == 0, partner, own)
    term = None
    for source, right in chip_cotangents(s0, s1, s2, far0, far1):
        left = jnp.concatenate(
            [
                jnp.concatenate([pair_ref[source * C + c, head] for head in range(C)], axis=1)
                for c in range(C)
            ],
            axis=0,
        )
        part = dot(left, right, 0, 0)
        term = part if term is None else term + part
    term = term.astype(BF)
    for y in range(Y):
        for h in range(H):
            for z in range(Z):
                row = (z * H + h) * ROWS
                term_ref[(y * H + h) * Z + z] = term[
                    row : row + ROWS, y * COLS : (y + 1) * COLS
                ]


def home_kernel(
    off_ref, heads_ref, scaled_ref, state_ref, att_ref, partner_ref, own_ref, e1, e2, e3, *refs
):
    outs, (gq, gk, gv) = refs[:X], refs[X:]
    plane = lax.axis_index("z")
    x = lax.axis_index("x")
    core = lax.axis_index("c")
    found = edge_utterances(off_ref, plane)
    key = heads_ref[:, 1].reshape(CHUNK, HD)
    value = heads_ref[:, 2].reshape(CHUNK, HD)
    scaled = scaled_ref[...]
    for u in range(UTTS):

        @pl.when(present(off_ref, u, plane))
        def _(u=u):
            grad = whole_sum(u, own_ref, (e1, e2, e3), 1, found)
            mask = row_mask(off_ref, u, plane)
            gq[...] = jnp.where(mask, dot(scaled, state_ref[u], 1, 1), gq[...])
            gk[...] = jnp.where(mask, dot(value, grad, 1, 1), gk[...])
            gv[...] = jnp.where(mask, dot(key, grad), gv[...])

    for shift, out in enumerate(outs):
        for c in range(C):
            block = lax.rem(x + shift, X) * C + c
            rows = pl.ds(pl.multiple_of(block * FRAMES, FRAMES), FRAMES)
            for place, ref in enumerate((gq, gk, gv)):
                out[c, place] = ref[rows, :].astype(BF)
            out[c, 3 + core] = att_ref[block]
            out[c, 4 - core] = partner_ref[block]


def encode_kernel(r0, r1, r2, r3, w0, w1, w2, top, bottom, keep_ref, give_ref):
    core = lax.axis_index("c")
    total = None
    weights = (w0[...], w1[...], w2[...], jnp.concatenate([top[...], bottom[...]], axis=0))
    for ref, weight, source in zip((r0, r1, r2, r3), weights, sources()):
        for place in range(3):
            keep_ref[source * 3 + place] = ref[core, place]
            give_ref[source * 3 + place] = ref[1 - core, place]
        left = jnp.concatenate(
            [jnp.concatenate([ref[c, 3], ref[c, 4]], axis=1) for c in range(C)], axis=0
        )
        part = dot(left, weight)
        total = part if total is None else total + part
    total = total.astype(BF)
    zero, one = total[:FRAMES], total[FRAMES:]
    mine = jnp.where(core == 0, zero, one)
    theirs = jnp.where(core == 0, one, zero)
    for tile in range(TILES):
        columns = slice(tile * HD, (tile + 1) * HD)
        keep_ref[X * 3 + tile] = mine[:, columns]
        give_ref[X * 3 + tile] = theirs[:, columns]


def finish_kernel(keep_ref, came_ref, enc_ref, q_ref, k_ref, v_ref):
    core = lax.axis_index("c")

    def place_all(parts):
        for c, part in enumerate(parts):
            for pair in range(X):
                start = (pair * C + c) * HD
                for place, ref in enumerate((q_ref, k_ref, v_ref)):
                    ref[0, :, start : start + HD] = part[pair * 3 + place]
            for tile in range(TILES):
                start = (tile // 2) * C * COLS + c * COLS + (tile % 2) * HD
                enc_ref[0, :, start : start + HD] = part[X * 3 + tile]

    @pl.when(core == 0)
    def _():
        place_all((keep_ref, came_ref))

    @pl.when(core == 1)
    def _():
        place_all((came_ref, keep_ref))


def flat(y, h, z, x, c):
    return (((y * H + h) * Z + z) * X + x) * C + c


def swap_pairs():
    return [
        (flat(y, h, z, x, c), flat(y, c, x, z, h))
        for y in range(Y)
        for h in range(H)
        for z in range(Z)
        for x in range(X)
        for c in range(C)
    ]


def turn(value, axis, size, shift):
    return lax.ppermute(value, axis, [(i, (i + shift) % size) for i in range(size)])


def swap_cores(value):
    return turn(value, "c", C, 1)


def body(queries, key_vectors, values, cotangent, out_weight, offsets):
    group = Y * H * Z
    state_shape = (UTTS, HD, HD)
    edge_shape = (2, HD, HD)
    side = (X * 3 + TILES, FRAMES, HD)
    chunk_scratch = pltpu.VMEM((CHUNK, HD), F32)

    moved = lax.ppermute(out_weight, ALL, swap_pairs())
    pieces = lax.all_to_all(
        jnp.broadcast_to(moved[None], (group, ROWS, COLS)), ACROSS, 0, 0, tiled=True
    )
    keep, give = call(
        prepare_kernel,
        [(side, BF)] * 2,
        queries,
        key_vectors,
        values,
        cotangent,
        scratch=[pltpu.SemaphoreType.DMA((2 * side[0],))],
        where=pl.ANY,
        mib=60,
    )
    s0, to_next, to_back = call(
        merge_kernel,
        [((C * PASSED, FRAMES, HD), BF)] + [((C * PASSED + 3, FRAMES, HD), BF)] * 2,
        keep,
        swap_cores(give),
        after=[moved],
    )
    s1, s2 = turn(to_next, "x", X, 1), turn(to_back, "x", X, -1)
    rows = (s0, s1, s2, turn(s1[:PASSED], "x", X, 1), turn(s2[:PASSED], "x", X, -1))

    (weight,) = call(block_kernel, [((2 * HD, HALF), BF)], pieces)
    w1, w2 = turn(weight, "x", X, 1), turn(weight, "x", X, -1)
    top, bottom = turn(w1[:HD], "x", X, 1), turn(w2[HD:], "x", X, -1)
    mine, theirs = call(
        cotangent_kernel, [((BLOCKS, FRAMES, HD), F32)] * 2, weight, *rows
    )
    heads, own, edge = call(
        state_kernel,
        [((BLOCKS, 3, FRAMES, HD), BF), (state_shape, F32), ((Z - 1, HD, HD), BF)],
        offsets,
        *rows,
        smem=1,
        after=[theirs],
    )
    scaled, gown, *edges = call(
        gradient_kernel,
        [((CHUNK, HD), BF), (state_shape, F32)] + [(edge_shape, BF)] * (Z - 1),
        offsets,
        heads,
        mine,
        swap_cores(theirs),
        edge,
        scratch=[chunk_scratch],
        smem=1,
    )
    edges = [turn(part, "z", Z, shift) for shift, part in enumerate(edges, 1)]
    attended, state = call(
        attended_kernel,
        [((BLOCKS, FRAMES, HD), BF), (state_shape, BF)],
        offsets,
        heads,
        own,
        *edges,
        scratch=[chunk_scratch],
        smem=1,
        after=[w1, w2],
    )
    partner = swap_cores(attended)
    r0, h1, h2, h3 = call(
        home_kernel,
        [((C, 5, FRAMES, HD), BF)] * X,
        offsets,
        heads,
        scaled,
        state,
        attended,
        partner,
        gown,
        *edges,
        scratch=[chunk_scratch] * 3,
        smem=1,
    )
    (term,) = call(
        weight_kernel,
        [((group, ROWS, COLS), BF)],
        attended,
        partner,
        *rows,
        scratch=[pltpu.VMEM((BLOCKS, C, FRAMES, HD), BF)],
        after=[r0, top, bottom],
    )
    term = lax.all_to_all(term, ACROSS, 0, 0, tiled=True)
    grad_weight = jnp.sum(term.astype(F32), axis=0) / math.sqrt(Y * H * LENGTH)
    grad_weight = lax.ppermute(grad_weight, ALL, swap_pairs())

    keep, give = call(
        encode_kernel,
        [(side, BF)] * 2,
        r0,
        turn(h1, "x", X, 1),
        turn(h3, "x", X, -1),
        turn(h2, "x", X, 2),
        weight,
        w1,
        w2,
        top,
        bottom,
    )
    encoded, *grads = call(
        finish_kernel,
        [((1, FRAMES, C * HALF), BF)] + [((1, FRAMES, BLOCKS * HD), BF)] * 3,
        keep,
        swap_cores(give),
    )
    return (encoded, grads[0], grads[1], grads[2], grad_weight)


def solution(mesh):
    fine = Mesh(np.asarray(mesh.devices).reshape(Y, H, Z, X, C), ALL)
    dp, tm = ("y", "h"), ("z", "x", "c")
    three = P(dp, tm, None)
    in_specs = (three, three, three, three, P(tm, dp), P(dp, None))
    out_specs = (three, three, three, three, P(tm, dp))
    return jax.shard_map(body, mesh=fine, in_specs=in_specs, out_specs=out_specs, check_vma=False)
```

```python
import math

import jax
import jax.numpy as jnp
import numpy as np
from jax import lax
from jax.experimental import pallas as pl
from jax.experimental.pallas import tpu as pltpu
from jax.sharding import Mesh
from jax.sharding import PartitionSpec as P

HD = 128
FRAMES = 128
Y, H, Z, X, C = 4, 2, 4, 4, 2
BLOCKS = X * C
CHUNK = BLOCKS * FRAMES
LENGTH = Z * CHUNK
UTTS = 12
ROWS = 32
COLS = 256
HALF = Y * COLS
TILES = HALF // HD
PASSED = TILES + 3
ALL = ("y", "h", "z", "x", "c")
ACROSS = ("y", "h", "z")
BF = jnp.bfloat16
F32 = jnp.float32

VMEM = pl.BlockSpec(memory_space=pltpu.VMEM)
SMEM = pl.BlockSpec(memory_space=pltpu.SMEM)


def call(kernel, outs, *args, scratch=(), smem=0, where=pltpu.VMEM, after=(), mib=40):
    count = len(args)

    def run(*refs):
        kernel(*refs[:count], *refs[count + len(after) :])

    specs = [SMEM] * smem + [pl.BlockSpec(memory_space=where)] * (count - smem)
    return pl.pallas_call(
        run,
        out_shape=[jax.ShapeDtypeStruct(shape, dtype) for shape, dtype in outs],
        in_specs=specs + [pl.BlockSpec(memory_space=pl.ANY)] * len(after),
        out_specs=[VMEM] * len(outs),
        scratch_shapes=list(scratch),
        compiler_params=pltpu.CompilerParams(vmem_limit_bytes=mib * 1024 * 1024),
    )(*args, *after)


def gate(value, after):
    anywhere = pl.BlockSpec(memory_space=pl.ANY)
    return pl.pallas_call(
        lambda *refs: None,
        out_shape=jax.ShapeDtypeStruct(value.shape, value.dtype),
        in_specs=[anywhere] * (1 + len(after)),
        out_specs=anywhere,
        input_output_aliases={0: 0},
    )(value, *after)


def dot(a, b, left=1, right=0):
    return lax.dot_general(
        a, b, (((left,), (right,)), ((), ())), preferred_element_type=F32
    )


def limits(off_ref, u, plane):
    base = plane * CHUNK
    end = off_ref[0, u + 1] if u + 1 < UTTS else LENGTH
    return off_ref[0, u] - base, end - base


def present(off_ref, u, plane):
    low, high = limits(off_ref, u, plane)
    return (low < CHUNK) & (high > 0)


def row_mask(off_ref, u, plane):
    low, high = limits(off_ref, u, plane)
    rows = lax.broadcasted_iota(jnp.int32, (CHUNK, HD), 0)
    return (rows >= low) & (rows < high)


def lane_mask(off_ref, u, plane):
    low, high = limits(off_ref, u, plane)
    lanes = lax.broadcasted_iota(jnp.int32, (HD, CHUNK), 1)
    return (lanes >= low) & (lanes < high)


def scale_of(off_ref, u, plane):
    low, high = limits(off_ref, u, plane)
    span = jnp.full((1, HD), HD * (high - low), jnp.int32).astype(F32)
    return 1.0 / jnp.sqrt(span)


def utterance_at(off_ref, frame):
    count = jnp.int32(-1)
    for u in range(UTTS):
        count = count + (off_ref[0, u] <= frame).astype(jnp.int32)
    return count


def partial_sums(off_ref, plane, left_t, right, own_ref):
    for u in range(UTTS):

        @pl.when(present(off_ref, u, plane))
        def _(u=u):
            masked = jnp.where(lane_mask(off_ref, u, plane), left_t, 0.0).astype(BF)
            own_ref[u] = dot(masked, right)

    first = utterance_at(off_ref, plane * CHUNK)
    last = utterance_at(off_ref, plane * CHUNK + CHUNK - 1)
    return [
        own_ref[jnp.where(plane + shift < Z, last, first)].astype(BF) for shift in range(1, Z)
    ]


def edge_utterances(off_ref, plane):
    found = []
    for shift in range(1, Z):
        source = lax.rem(plane + Z - shift, Z)
        frame = source * CHUNK + jnp.where(source < plane, CHUNK - 1, 0)
        found.append(utterance_at(off_ref, frame))
    return found


def whole_sum(u, own_ref, edge_refs, which, found):
    total = own_ref[u]
    for edge_ref, utterance in zip(edge_refs, found):
        total = total + edge_ref[which].astype(F32) * (utterance == u).astype(F32)
    return total.astype(BF)


def prepare_kernel(q_ref, k_ref, v_ref, cot_ref, keep_ref, give_ref, sems):
    core = lax.axis_index("c")
    copies = []
    for side, (ref, whose) in enumerate(((give_ref, 1 - core), (keep_ref, core))):
        for pair in range(X):
            start = pl.multiple_of((pair * C + whose) * HD, HD)
            for place, source in enumerate((q_ref, k_ref, v_ref)):
                copies.append((source.at[0, :, pl.ds(start, HD)], ref.at[pair * 3 + place], side))
        for tile in range(TILES):
            start = (tile // 2) * C * COLS + whose * COLS + (tile % 2) * HD
            start = pl.multiple_of(start, HD)
            copies.append((cot_ref.at[0, :, pl.ds(start, HD)], ref.at[X * 3 + tile], side))
    copies = [
        pltpu.make_async_copy(source, target, sems.at[i])
        for i, (source, target, _) in enumerate(copies)
    ]
    for copy in copies:
        copy.start()
    for copy in copies:
        copy.wait()


def merge_kernel(keep_ref, came_ref, self_ref, next_ref, back_ref):
    core = lax.axis_index("c")
    x = lax.axis_index("x")
    far = lax.rem(x + 2, X) * 3
    for mine, block in ((keep_ref, core), (came_ref, 1 - core)):
        for first, out, shift in ((0, next_ref, 1), (1, back_ref, 3)):
            near = lax.rem(x + shift, X) * 3
            cot = jnp.where(block == first, 0, PASSED)
            out[pl.ds(cot, TILES)] = mine[X * 3 :]
            out[pl.ds(PASSED + TILES + block * 3, 3)] = mine[pl.ds(near, 3)]

            @pl.when(block == first)
            def _(mine=mine, out=out):
                out[TILES:PASSED] = mine[pl.ds(far, 3)]

        self_ref[pl.ds(block * TILES, TILES)] = mine[X * 3 :]
        self_ref[pl.ds(C * TILES + block * 3, 3)] = mine[pl.ds(x * 3, 3)]


def sources():
    x = lax.axis_index("x")
    return (x, lax.rem(x + X - 1, X), lax.rem(x + 1, X), lax.rem(x + 2, X))


def state_kernel(off_ref, s0, s1, s2, far0, far1, heads_ref, own_ref, edge_ref):
    plane = lax.axis_index("z")
    parts = [[ref[start : start + 3] for start in starts] for ref, starts in (
        (s0, (C * TILES, C * TILES + 3)),
        (s1, (PASSED + TILES, PASSED + TILES + 3)),
        (s2, (PASSED + TILES, PASSED + TILES + 3)),
    )]
    parts.append([far0[TILES:], far1[TILES:]])
    for pair, source in zip(parts, sources()):
        for core, part in enumerate(pair):
            heads_ref[source * C + core] = part
    key = heads_ref[:, 1].reshape(CHUNK, HD).astype(F32)
    value = heads_ref[:, 2].reshape(CHUNK, HD)
    edges = partial_sums(off_ref, plane, key.T, value, own_ref)
    for place, edge in enumerate(edges):
        edge_ref[place] = edge


def attended_kernel(off_ref, heads_ref, own_ref, e1, e2, e3, attended_ref, state_ref, total_ref):
    plane = lax.axis_index("z")
    found = edge_utterances(off_ref, plane)
    query = heads_ref[:, 0].reshape(CHUNK, HD)
    for u in range(UTTS):

        @pl.when(present(off_ref, u, plane))
        def _(u=u):
            state = whole_sum(u, own_ref, (e1, e2, e3), 0, found)
            state_ref[u] = state
            rows = dot(query, state) * scale_of(off_ref, u, plane)
            total_ref[...] = jnp.where(row_mask(off_ref, u, plane), rows, total_ref[...])

    attended_ref[...] = total_ref[...].astype(BF).reshape(BLOCKS, FRAMES, HD)


def wide(tiles):
    return jnp.concatenate([tiles[i] for i in range(TILES)], axis=1)


def chip_cotangents(s0, s1, s2, far0, far1):
    parts = (
        (s0[:TILES], s0[TILES : 2 * TILES]),
        (s1[:TILES], s1[PASSED : PASSED + TILES]),
        (s2[PASSED : PASSED + TILES], s2[:TILES]),
        (far0[:TILES], far1[:TILES]),
    )
    for pair, source in zip(parts, sources()):
        yield source, jnp.concatenate([wide(part) for part in pair], axis=0)


def block_kernel(pieces_ref, weight_ref):
    for y in range(Y):
        for h in range(H):
            for z in range(Z):
                row = (z * H + h) * ROWS
                weight_ref[row : row + ROWS, y * COLS : (y + 1) * COLS] = pieces_ref[
                    (y * H + h) * Z + z
                ]


def cotangent_kernel(weight_ref, s0, s1, s2, far0, far1, mine_ref, theirs_ref):
    core = lax.axis_index("c")
    weight = weight_ref[...]
    for source, rows in chip_cotangents(s0, s1, s2, far0, far1):
        back = dot(rows, weight, 1, 1)
        low, high = back[:, :HD], back[:, HD:]
        mine = jnp.where(core == 0, low, high)
        theirs = jnp.where(core == 0, high, low)
        for c in range(C):
            mine_ref[source * C + c] = mine[c * FRAMES : (c + 1) * FRAMES]
            theirs_ref[source * C + c] = theirs[c * FRAMES : (c + 1) * FRAMES]


def gradient_kernel(
    off_ref, heads_ref, mine_ref, came_ref, edge_ref, scaled_ref, own_ref, o1, o2, o3, total_ref
):
    plane = lax.axis_index("z")
    back = (mine_ref[...] + came_ref[...]).reshape(CHUNK, HD)
    for u in range(UTTS):

        @pl.when(present(off_ref, u, plane))
        def _(u=u):
            rows = back * scale_of(off_ref, u, plane)
            total_ref[...] = jnp.where(row_mask(off_ref, u, plane), rows, total_ref[...])

    scaled = total_ref[...].astype(BF)
    scaled_ref[...] = scaled
    query = heads_ref[:, 0].reshape(CHUNK, HD).astype(F32)
    edges = partial_sums(off_ref, plane, query.T, scaled, own_ref)
    for place, (edge, out) in enumerate(zip(edges, (o1, o2, o3))):
        out[0] = edge_ref[place]
        out[1] = edge


def weight_kernel(own_ref, partner_ref, s0, s1, s2, far0, far1, term_ref, pair_ref):
    core = lax.axis_index("c")
    own, partner = own_ref[...], partner_ref[...]
    pair_ref[:, 0] = jnp.where(core == 0, own, partner)
    pair_ref[:, 1] = jnp.where(core == 0, partner, own)
    term = None
    for source, right in chip_cotangents(s0, s1, s2, far0, far1):
        left = jnp.concatenate(
            [
                jnp.concatenate([pair_ref[source * C + c, head] for head in range(C)], axis=1)
                for c in range(C)
            ],
            axis=0,
        )
        part = dot(left, right, 0, 0)
        term = part if term is None else term + part
    term = term.astype(BF)
    for y in range(Y):
        for h in range(H):
            for z in range(Z):
                row = (z * H + h) * ROWS
                term_ref[(y * H + h) * Z + z] = term[
                    row : row + ROWS, y * COLS : (y + 1) * COLS
                ]


def home_kernel(
    off_ref, heads_ref, scaled_ref, state_ref, att_ref, partner_ref, own_ref, e1, e2, e3, *refs
):
    outs, (gq, gk, gv) = refs[:X], refs[X:]
    plane = lax.axis_index("z")
    x = lax.axis_index("x")
    core = lax.axis_index("c")
    found = edge_utterances(off_ref, plane)
    key = heads_ref[:, 1].reshape(CHUNK, HD)
    value = heads_ref[:, 2].reshape(CHUNK, HD)
    scaled = scaled_ref[...]
    for u in range(UTTS):

        @pl.when(present(off_ref, u, plane))
        def _(u=u):
            grad = whole_sum(u, own_ref, (e1, e2, e3), 1, found)
            mask = row_mask(off_ref, u, plane)
            gq[...] = jnp.where(mask, dot(scaled, state_ref[u], 1, 1), gq[...])
            gk[...] = jnp.where(mask, dot(value, grad, 1, 1), gk[...])
            gv[...] = jnp.where(mask, dot(key, grad), gv[...])

    for shift, out in enumerate(outs):
        for c in range(C):
            block = lax.rem(x + shift, X) * C + c
            rows = pl.ds(pl.multiple_of(block * FRAMES, FRAMES), FRAMES)
            for place, ref in enumerate((gq, gk, gv)):
                out[c, place] = ref[rows, :].astype(BF)
            out[c, 3 + core] = att_ref[block]
            out[c, 4 - core] = partner_ref[block]


def encode_kernel(r0, r1, r2, r3, w0, w1, w2, top, bottom, keep_ref, give_ref):
    core = lax.axis_index("c")
    total = None
    weights = (w0[...], w1[...], w2[...], jnp.concatenate([top[...], bottom[...]], axis=0))
    for ref, weight, source in zip((r0, r1, r2, r3), weights, sources()):
        for place in range(3):
            keep_ref[source * 3 + place] = ref[core, place]
            give_ref[source * 3 + place] = ref[1 - core, place]
        left = jnp.concatenate(
            [jnp.concatenate([ref[c, 3], ref[c, 4]], axis=1) for c in range(C)], axis=0
        )
        part = dot(left, weight)
        total = part if total is None else total + part
    total = total.astype(BF)
    zero, one = total[:FRAMES], total[FRAMES:]
    mine = jnp.where(core == 0, zero, one)
    theirs = jnp.where(core == 0, one, zero)
    for tile in range(TILES):
        columns = slice(tile * HD, (tile + 1) * HD)
        keep_ref[X * 3 + tile] = mine[:, columns]
        give_ref[X * 3 + tile] = theirs[:, columns]


def finish_kernel(keep_ref, came_ref, enc_ref, q_ref, k_ref, v_ref):
    core = lax.axis_index("c")

    def place_all(parts):
        for c, part in enumerate(parts):
            for pair in range(X):
                start = (pair * C + c) * HD
                for place, ref in enumerate((q_ref, k_ref, v_ref)):
                    ref[0, :, start : start + HD] = part[pair * 3 + place]
            for tile in range(TILES):
                start = (tile // 2) * C * COLS + c * COLS + (tile % 2) * HD
                enc_ref[0, :, start : start + HD] = part[X * 3 + tile]

    @pl.when(core == 0)
    def _():
        place_all((keep_ref, came_ref))

    @pl.when(core == 1)
    def _():
        place_all((came_ref, keep_ref))


def flat(y, h, z, x, c):
    return (((y * H + h) * Z + z) * X + x) * C + c


def swap_pairs():
    return [
        (flat(y, h, z, x, c), flat(y, c, x, z, h))
        for y in range(Y)
        for h in range(H)
        for z in range(Z)
        for x in range(X)
        for c in range(C)
    ]


def turn(value, axis, size, shift):
    return lax.ppermute(value, axis, [(i, (i + shift) % size) for i in range(size)])


def swap_cores(value):
    return turn(value, "c", C, 1)


def body(queries, key_vectors, values, cotangent, out_weight, offsets):
    group = Y * H * Z
    state_shape = (UTTS, HD, HD)
    edge_shape = (2, HD, HD)
    side = (X * 3 + TILES, FRAMES, HD)
    chunk_scratch = pltpu.VMEM((CHUNK, HD), F32)

    moved = lax.ppermute(out_weight, ALL, swap_pairs())
    pieces = lax.all_to_all(
        jnp.broadcast_to(moved[None], (group, ROWS, COLS)), ACROSS, 0, 0, tiled=True
    )
    keep, give = call(
        prepare_kernel,
        [(side, BF)] * 2,
        queries,
        key_vectors,
        values,
        cotangent,
        scratch=[pltpu.SemaphoreType.DMA((2 * side[0],))],
        where=pl.ANY,
        mib=60,
    )
    s0, to_next, to_back = call(
        merge_kernel,
        [((C * PASSED, FRAMES, HD), BF)] + [((C * PASSED + 3, FRAMES, HD), BF)] * 2,
        keep,
        swap_cores(give),
    )
    s1, s2 = turn(to_next, "x", X, 1), turn(to_back, "x", X, -1)
    rows = (s0, s1, s2, turn(s1[:PASSED], "x", X, 1), turn(s2[:PASSED], "x", X, -1))

    (weight,) = call(block_kernel, [((2 * HD, HALF), BF)], pieces)
    w1, w2 = turn(weight, "x", X, 1), turn(weight, "x", X, -1)
    top, bottom = turn(w1[:HD], "x", X, 1), turn(w2[HD:], "x", X, -1)
    mine, theirs = call(
        cotangent_kernel, [((BLOCKS, FRAMES, HD), F32)] * 2, weight, *rows
    )
    heads, own, edge = call(
        state_kernel,
        [((BLOCKS, 3, FRAMES, HD), BF), (state_shape, F32), ((Z - 1, HD, HD), BF)],
        offsets,
        *rows,
        smem=1,
        after=[theirs],
    )
    scaled, gown, *edges = call(
        gradient_kernel,
        [((CHUNK, HD), BF), (state_shape, F32)] + [(edge_shape, BF)] * (Z - 1),
        offsets,
        heads,
        mine,
        swap_cores(theirs),
        edge,
        scratch=[chunk_scratch],
        smem=1,
    )
    edges = [turn(part, "z", Z, shift) for shift, part in enumerate(edges, 1)]
    attended, state = call(
        attended_kernel,
        [((BLOCKS, FRAMES, HD), BF), (state_shape, BF)],
        offsets,
        heads,
        own,
        *edges,
        scratch=[chunk_scratch],
        smem=1,
        after=[w1, w2],
    )
    partner = swap_cores(attended)
    r0, h1, h2, h3 = call(
        home_kernel,
        [((C, 5, FRAMES, HD), BF)] * X,
        offsets,
        heads,
        scaled,
        state,
        attended,
        partner,
        gown,
        *edges,
        scratch=[chunk_scratch] * 3,
        smem=1,
        after=[top, bottom],
    )
    (term,) = call(
        weight_kernel,
        [((group, ROWS, COLS), BF)],
        attended,
        partner,
        *rows,
        scratch=[pltpu.VMEM((BLOCKS, C, FRAMES, HD), BF)],
    )
    h1, h2, h3 = turn(h1, "x", X, 1), turn(h2, "x", X, 2), turn(h3, "x", X, -1)
    term = lax.all_to_all(gate(term, [r0]), ACROSS, 0, 0, tiled=True)
    grad_weight = jnp.sum(term.astype(F32), axis=0) / math.sqrt(Y * H * LENGTH)
    grad_weight = lax.ppermute(grad_weight, ALL, swap_pairs())

    keep, give = call(
        encode_kernel,
        [(side, BF)] * 2,
        r0,
        h1,
        h3,
        h2,
        weight,
        w1,
        w2,
        top,
        bottom,
    )
    encoded, *grads = call(
        finish_kernel,
        [((1, FRAMES, C * HALF), BF)] + [((1, FRAMES, BLOCKS * HD), BF)] * 3,
        keep,
        swap_cores(give),
    )
    return (encoded, grads[0], grads[1], grads[2], grad_weight)


def solution(mesh):
    fine = Mesh(np.asarray(mesh.devices).reshape(Y, H, Z, X, C), ALL)
    dp, tm = ("y", "h"), ("z", "x", "c")
    three = P(dp, tm, None)
    in_specs = (three, three, three, three, P(tm, dp), P(dp, None))
    out_specs = (three, three, three, three, P(tm, dp))
    return jax.shard_map(body, mesh=fine, in_specs=in_specs, out_specs=out_specs, check_vma=False)
```

```python
import math

import jax
import jax.numpy as jnp
import numpy as np
from jax import lax
from jax.experimental import pallas as pl
from jax.experimental.pallas import tpu as pltpu
from jax.sharding import Mesh
from jax.sharding import PartitionSpec as P

HD = 128
FRAMES = 128
Y, H, Z, X, C = 4, 2, 4, 4, 2
BLOCKS = X * C
CHUNK = BLOCKS * FRAMES
LENGTH = Z * CHUNK
UTTS = 12
ROWS = 32
COLS = 256
HALF = Y * COLS
TILES = HALF // HD
PASSED = TILES + 3
ALL = ("y", "h", "z", "x", "c")
ACROSS = ("y", "h", "z")
BF = jnp.bfloat16
F32 = jnp.float32

VMEM = pl.BlockSpec(memory_space=pltpu.VMEM)
SMEM = pl.BlockSpec(memory_space=pltpu.SMEM)


def call(kernel, outs, *args, scratch=(), smem=0, where=pltpu.VMEM, after=(), mib=40):
    count = len(args)

    def run(*refs):
        kernel(*refs[:count], *refs[count + len(after) :])

    specs = [SMEM] * smem + [pl.BlockSpec(memory_space=where)] * (count - smem)
    return pl.pallas_call(
        run,
        out_shape=[jax.ShapeDtypeStruct(shape, dtype) for shape, dtype in outs],
        in_specs=specs + [pl.BlockSpec(memory_space=pl.ANY)] * len(after),
        out_specs=[VMEM] * len(outs),
        scratch_shapes=list(scratch),
        compiler_params=pltpu.CompilerParams(vmem_limit_bytes=mib * 1024 * 1024),
    )(*args, *after)


def gate(value, after):
    anywhere = pl.BlockSpec(memory_space=pl.ANY)
    return pl.pallas_call(
        lambda *refs: None,
        out_shape=jax.ShapeDtypeStruct(value.shape, value.dtype),
        in_specs=[anywhere] * (1 + len(after)),
        out_specs=anywhere,
        input_output_aliases={0: 0},
    )(value, *after)


def dot(a, b, left=1, right=0):
    return lax.dot_general(
        a, b, (((left,), (right,)), ((), ())), preferred_element_type=F32
    )


def limits(off_ref, u, plane):
    base = plane * CHUNK
    end = off_ref[0, u + 1] if u + 1 < UTTS else LENGTH
    return off_ref[0, u] - base, end - base


def present(off_ref, u, plane):
    low, high = limits(off_ref, u, plane)
    return (low < CHUNK) & (high > 0)


def row_mask(off_ref, u, plane):
    low, high = limits(off_ref, u, plane)
    rows = lax.broadcasted_iota(jnp.int32, (CHUNK, HD), 0)
    return (rows >= low) & (rows < high)


def lane_mask(off_ref, u, plane):
    low, high = limits(off_ref, u, plane)
    lanes = lax.broadcasted_iota(jnp.int32, (HD, CHUNK), 1)
    return (lanes >= low) & (lanes < high)


def scale_of(off_ref, u, plane):
    low, high = limits(off_ref, u, plane)
    span = jnp.full((1, HD), HD * (high - low), jnp.int32).astype(F32)
    return 1.0 / jnp.sqrt(span)


def utterance_at(off_ref, frame):
    count = jnp.int32(-1)
    for u in range(UTTS):
        count = count + (off_ref[0, u] <= frame).astype(jnp.int32)
    return count


def partial_sums(off_ref, plane, left_t, right, own_ref):
    for u in range(UTTS):

        @pl.when(present(off_ref, u, plane))
        def _(u=u):
            masked = jnp.where(lane_mask(off_ref, u, plane), left_t, 0.0).astype(BF)
            own_ref[u] = dot(masked, right)

    first = utterance_at(off_ref, plane * CHUNK)
    last = utterance_at(off_ref, plane * CHUNK + CHUNK - 1)
    return [
        own_ref[jnp.where(plane + shift < Z, last, first)].astype(BF) for shift in range(1, Z)
    ]


def edge_utterances(off_ref, plane):
    found = []
    for shift in range(1, Z):
        source = lax.rem(plane + Z - shift, Z)
        frame = source * CHUNK + jnp.where(source < plane, CHUNK - 1, 0)
        found.append(utterance_at(off_ref, frame))
    return found


def whole_sum(u, own_ref, edge_refs, which, found):
    total = own_ref[u]
    for edge_ref, utterance in zip(edge_refs, found):
        total = total + edge_ref[which].astype(F32) * (utterance == u).astype(F32)
    return total.astype(BF)


def prepare_kernel(q_ref, k_ref, v_ref, cot_ref, keep_ref, give_ref, sems):
    core = lax.axis_index("c")
    copies = []
    for side, (ref, whose) in enumerate(((give_ref, 1 - core), (keep_ref, core))):
        for pair in range(X):
            start = pl.multiple_of((pair * C + whose) * HD, HD)
            for place, source in enumerate((q_ref, k_ref, v_ref)):
                copies.append((source.at[0, :, pl.ds(start, HD)], ref.at[pair * 3 + place], side))
        for tile in range(TILES):
            start = (tile // 2) * C * COLS + whose * COLS + (tile % 2) * HD
            start = pl.multiple_of(start, HD)
            copies.append((cot_ref.at[0, :, pl.ds(start, HD)], ref.at[X * 3 + tile], side))
    copies = [
        pltpu.make_async_copy(source, target, sems.at[i])
        for i, (source, target, _) in enumerate(copies)
    ]
    for copy in copies:
        copy.start()
    for copy in copies:
        copy.wait()


def merge_kernel(keep_ref, came_ref, self_ref, next_ref, back_ref):
    core = lax.axis_index("c")
    x = lax.axis_index("x")
    far = lax.rem(x + 2, X) * 3
    for mine, block in ((keep_ref, core), (came_ref, 1 - core)):
        for first, out, shift in ((0, next_ref, 1), (1, back_ref, 3)):
            near = lax.rem(x + shift, X) * 3
            cot = jnp.where(block == first, 0, PASSED)
            out[pl.ds(cot, TILES)] = mine[X * 3 :]
            out[pl.ds(PASSED + TILES + block * 3, 3)] = mine[pl.ds(near, 3)]

            @pl.when(block == first)
            def _(mine=mine, out=out):
                out[TILES:PASSED] = mine[pl.ds(far, 3)]

        self_ref[pl.ds(block * TILES, TILES)] = mine[X * 3 :]
        self_ref[pl.ds(C * TILES + block * 3, 3)] = mine[pl.ds(x * 3, 3)]


def sources():
    x = lax.axis_index("x")
    return (x, lax.rem(x + X - 1, X), lax.rem(x + 1, X), lax.rem(x + 2, X))


def state_kernel(off_ref, s0, s1, s2, far0, far1, heads_ref, own_ref, edge_ref):
    plane = lax.axis_index("z")
    parts = [[ref[start : start + 3] for start in starts] for ref, starts in (
        (s0, (C * TILES, C * TILES + 3)),
        (s1, (PASSED + TILES, PASSED + TILES + 3)),
        (s2, (PASSED + TILES, PASSED + TILES + 3)),
    )]
    parts.append([far0[TILES:], far1[TILES:]])
    for pair, source in zip(parts, sources()):
        for core, part in enumerate(pair):
            heads_ref[source * C + core] = part
    key = heads_ref[:, 1].reshape(CHUNK, HD).astype(F32)
    value = heads_ref[:, 2].reshape(CHUNK, HD)
    edges = partial_sums(off_ref, plane, key.T, value, own_ref)
    for place, edge in enumerate(edges):
        edge_ref[place] = edge


def attended_kernel(off_ref, heads_ref, own_ref, e1, e2, e3, attended_ref, state_ref, total_ref):
    plane = lax.axis_index("z")
    found = edge_utterances(off_ref, plane)
    query = heads_ref[:, 0].reshape(CHUNK, HD)
    for u in range(UTTS):

        @pl.when(present(off_ref, u, plane))
        def _(u=u):
            state = whole_sum(u, own_ref, (e1, e2, e3), 0, found)
            state_ref[u] = state
            rows = dot(query, state) * scale_of(off_ref, u, plane)
            total_ref[...] = jnp.where(row_mask(off_ref, u, plane), rows, total_ref[...])

    attended_ref[...] = total_ref[...].astype(BF).reshape(BLOCKS, FRAMES, HD)


def wide(tiles):
    return jnp.concatenate([tiles[i] for i in range(TILES)], axis=1)


def chip_cotangents(s0, s1, s2, far0, far1):
    parts = (
        (s0[:TILES], s0[TILES : 2 * TILES]),
        (s1[:TILES], s1[PASSED : PASSED + TILES]),
        (s2[PASSED : PASSED + TILES], s2[:TILES]),
        (far0[:TILES], far1[:TILES]),
    )
    for pair, source in zip(parts, sources()):
        yield source, jnp.concatenate([wide(part) for part in pair], axis=0)


def cotangent_kernel(pieces_ref, s0, s1, s2, far0, far1, mine_ref, theirs_ref, weight_ref):
    core = lax.axis_index("c")
    for y in range(Y):
        for h in range(H):
            for z in range(Z):
                row = (z * H + h) * ROWS
                weight_ref[row : row + ROWS, y * COLS : (y + 1) * COLS] = pieces_ref[
                    (y * H + h) * Z + z
                ]
    weight = weight_ref[...]
    for source, rows in chip_cotangents(s0, s1, s2, far0, far1):
        back = dot(rows, weight, 1, 1)
        low, high = back[:, :HD], back[:, HD:]
        mine = jnp.where(core == 0, low, high)
        theirs = jnp.where(core == 0, high, low)
        for c in range(C):
            mine_ref[source * C + c] = mine[c * FRAMES : (c + 1) * FRAMES]
            theirs_ref[source * C + c] = theirs[c * FRAMES : (c + 1) * FRAMES]


def gradient_kernel(
    off_ref, heads_ref, mine_ref, came_ref, edge_ref, scaled_ref, own_ref, o1, o2, o3, total_ref
):
    plane = lax.axis_index("z")
    back = (mine_ref[...] + came_ref[...]).reshape(CHUNK, HD)
    for u in range(UTTS):

        @pl.when(present(off_ref, u, plane))
        def _(u=u):
            rows = back * scale_of(off_ref, u, plane)
            total_ref[...] = jnp.where(row_mask(off_ref, u, plane), rows, total_ref[...])

    scaled = total_ref[...].astype(BF)
    scaled_ref[...] = scaled
    query = heads_ref[:, 0].reshape(CHUNK, HD).astype(F32)
    edges = partial_sums(off_ref, plane, query.T, scaled, own_ref)
    for place, (edge, out) in enumerate(zip(edges, (o1, o2, o3))):
        out[0] = edge_ref[place]
        out[1] = edge


def weight_kernel(own_ref, partner_ref, s0, s1, s2, far0, far1, term_ref, pair_ref):
    core = lax.axis_index("c")
    own, partner = own_ref[...], partner_ref[...]
    pair_ref[:, 0] = jnp.where(core == 0, own, partner)
    pair_ref[:, 1] = jnp.where(core == 0, partner, own)
    term = None
    for source, right in chip_cotangents(s0, s1, s2, far0, far1):
        left = jnp.concatenate(
            [
                jnp.concatenate([pair_ref[source * C + c, head] for head in range(C)], axis=1)
                for c in range(C)
            ],
            axis=0,
        )
        part = dot(left, right, 0, 0)
        term = part if term is None else term + part
    term = term.astype(BF)
    for y in range(Y):
        for h in range(H):
            for z in range(Z):
                row = (z * H + h) * ROWS
                term_ref[(y * H + h) * Z + z] = term[
                    row : row + ROWS, y * COLS : (y + 1) * COLS
                ]


def home_kernel(
    off_ref, heads_ref, scaled_ref, state_ref, att_ref, partner_ref, own_ref, e1, e2, e3, *refs
):
    outs, (gq, gk, gv) = refs[:X], refs[X:]
    plane = lax.axis_index("z")
    x = lax.axis_index("x")
    core = lax.axis_index("c")
    found = edge_utterances(off_ref, plane)
    key = heads_ref[:, 1].reshape(CHUNK, HD)
    value = heads_ref[:, 2].reshape(CHUNK, HD)
    scaled = scaled_ref[...]
    for u in range(UTTS):

        @pl.when(present(off_ref, u, plane))
        def _(u=u):
            grad = whole_sum(u, own_ref, (e1, e2, e3), 1, found)
            mask = row_mask(off_ref, u, plane)
            gq[...] = jnp.where(mask, dot(scaled, state_ref[u], 1, 1), gq[...])
            gk[...] = jnp.where(mask, dot(value, grad, 1, 1), gk[...])
            gv[...] = jnp.where(mask, dot(key, grad), gv[...])

    for shift, out in enumerate(outs):
        for c in range(C):
            block = lax.rem(x + shift, X) * C + c
            rows = pl.ds(pl.multiple_of(block * FRAMES, FRAMES), FRAMES)
            for place, ref in enumerate((gq, gk, gv)):
                out[c, place] = ref[rows, :].astype(BF)
            out[c, 3 + core] = att_ref[block]
            out[c, 4 - core] = partner_ref[block]


def encode_kernel(r0, r1, r2, r3, w0, w1, w2, top, bottom, keep_ref, give_ref):
    core = lax.axis_index("c")
    total = None
    weights = (w0[...], w1[...], w2[...], jnp.concatenate([top[...], bottom[...]], axis=0))
    for ref, weight, source in zip((r0, r1, r2, r3), weights, sources()):
        for place in range(3):
            keep_ref[source * 3 + place] = ref[core, place]
            give_ref[source * 3 + place] = ref[1 - core, place]
        left = jnp.concatenate(
            [jnp.concatenate([ref[c, 3], ref[c, 4]], axis=1) for c in range(C)], axis=0
        )
        part = dot(left, weight)
        total = part if total is None else total + part
    total = total.astype(BF)
    zero, one = total[:FRAMES], total[FRAMES:]
    mine = jnp.where(core == 0, zero, one)
    theirs = jnp.where(core == 0, one, zero)
    for tile in range(TILES):
        columns = slice(tile * HD, (tile + 1) * HD)
        keep_ref[X * 3 + tile] = mine[:, columns]
        give_ref[X * 3 + tile] = theirs[:, columns]


def finish_kernel(keep_ref, came_ref, enc_ref, q_ref, k_ref, v_ref):
    core = lax.axis_index("c")

    def place_all(parts):
        for c, part in enumerate(parts):
            for pair in range(X):
                start = (pair * C + c) * HD
                for place, ref in enumerate((q_ref, k_ref, v_ref)):
                    ref[0, :, start : start + HD] = part[pair * 3 + place]
            for tile in range(TILES):
                start = (tile // 2) * C * COLS + c * COLS + (tile % 2) * HD
                enc_ref[0, :, start : start + HD] = part[X * 3 + tile]

    @pl.when(core == 0)
    def _():
        place_all((keep_ref, came_ref))

    @pl.when(core == 1)
    def _():
        place_all((came_ref, keep_ref))


def flat(y, h, z, x, c):
    return (((y * H + h) * Z + z) * X + x) * C + c


def swap_pairs():
    return [
        (flat(y, h, z, x, c), flat(y, c, x, z, h))
        for y in range(Y)
        for h in range(H)
        for z in range(Z)
        for x in range(X)
        for c in range(C)
    ]


def turn(value, axis, size, shift):
    return lax.ppermute(value, axis, [(i, (i + shift) % size) for i in range(size)])


def swap_cores(value):
    return turn(value, "c", C, 1)


def body(queries, key_vectors, values, cotangent, out_weight, offsets):
    group = Y * H * Z
    state_shape = (UTTS, HD, HD)
    edge_shape = (2, HD, HD)
    side = (X * 3 + TILES, FRAMES, HD)
    chunk_scratch = pltpu.VMEM((CHUNK, HD), F32)

    moved = lax.ppermute(out_weight, ALL, swap_pairs())
    pieces = lax.all_to_all(
        jnp.broadcast_to(moved[None], (group, ROWS, COLS)), ACROSS, 0, 0, tiled=True
    )
    keep, give = call(
        prepare_kernel,
        [(side, BF)] * 2,
        queries,
        key_vectors,
        values,
        cotangent,
        scratch=[pltpu.SemaphoreType.DMA((2 * side[0],))],
        where=pl.ANY,
        mib=60,
    )
    s0, to_next, to_back = call(
        merge_kernel,
        [((C * PASSED, FRAMES, HD), BF)] + [((C * PASSED + 3, FRAMES, HD), BF)] * 2,
        keep,
        swap_cores(give),
    )
    s1, s2 = turn(to_next, "x", X, 1), turn(to_back, "x", X, -1)
    rows = (s0, s1, s2, turn(s1[:PASSED], "x", X, 1), turn(s2[:PASSED], "x", X, -1))

    mine, theirs, weight = call(
        cotangent_kernel,
        [((BLOCKS, FRAMES, HD), F32)] * 2 + [((2 * HD, HALF), BF)],
        pieces,
        *rows,
    )
    w1, w2 = turn(weight, "x", X, 1), turn(weight, "x", X, -1)
    top, bottom = turn(w1[:HD], "x", X, 1), turn(w2[HD:], "x", X, -1)
    heads, own, edge = call(
        state_kernel,
        [((BLOCKS, 3, FRAMES, HD), BF), (state_shape, F32), ((Z - 1, HD, HD), BF)],
        offsets,
        *rows,
        smem=1,
        after=[theirs],
    )
    scaled, gown, *edges = call(
        gradient_kernel,
        [((CHUNK, HD), BF), (state_shape, F32)] + [(edge_shape, BF)] * (Z - 1),
        offsets,
        heads,
        mine,
        swap_cores(theirs),
        edge,
        scratch=[chunk_scratch],
        smem=1,
    )
    edges = [turn(part, "z", Z, shift) for shift, part in enumerate(edges, 1)]
    attended, state = call(
        attended_kernel,
        [((BLOCKS, FRAMES, HD), BF), (state_shape, BF)],
        offsets,
        heads,
        own,
        *edges,
        scratch=[chunk_scratch],
        smem=1,
        after=[w1, w2],
    )
    partner = swap_cores(attended)
    r0, h1, h2, h3 = call(
        home_kernel,
        [((C, 5, FRAMES, HD), BF)] * X,
        offsets,
        heads,
        scaled,
        state,
        attended,
        partner,
        gown,
        *edges,
        scratch=[chunk_scratch] * 3,
        smem=1,
        after=[top, bottom],
    )
    (term,) = call(
        weight_kernel,
        [((group, ROWS, COLS), BF)],
        attended,
        partner,
        *rows,
        scratch=[pltpu.VMEM((BLOCKS, C, FRAMES, HD), BF)],
    )
    h1, h2, h3 = turn(h1, "x", X, 1), turn(h2, "x", X, 2), turn(h3, "x", X, -1)
    term = lax.all_to_all(gate(term, [r0]), ACROSS, 0, 0, tiled=True)
    grad_weight = jnp.sum(term.astype(F32), axis=0) / math.sqrt(Y * H * LENGTH)
    grad_weight = lax.ppermute(grad_weight, ALL, swap_pairs())

    keep, give = call(
        encode_kernel,
        [(side, BF)] * 2,
        r0,
        h1,
        h3,
        h2,
        weight,
        w1,
        w2,
        top,
        bottom,
    )
    encoded, *grads = call(
        finish_kernel,
        [((1, FRAMES, C * HALF), BF)] + [((1, FRAMES, BLOCKS * HD), BF)] * 3,
        keep,
        swap_cores(give),
    )
    return (encoded, grads[0], grads[1], grads[2], grad_weight)


def solution(mesh):
    fine = Mesh(np.asarray(mesh.devices).reshape(Y, H, Z, X, C), ALL)
    dp, tm = ("y", "h"), ("z", "x", "c")
    three = P(dp, tm, None)
    in_specs = (three, three, three, three, P(tm, dp), P(dp, None))
    out_specs = (three, three, three, three, P(tm, dp))
    return jax.shard_map(body, mesh=fine, in_specs=in_specs, out_specs=out_specs, check_vma=False)
```

```python
import math

import jax
import jax.numpy as jnp
import numpy as np
from jax import lax
from jax.experimental import pallas as pl
from jax.experimental.pallas import tpu as pltpu
from jax.sharding import Mesh
from jax.sharding import PartitionSpec as P

HD = 128
FRAMES = 128
Y, H, Z, X, C = 4, 2, 4, 4, 2
BLOCKS = X * C
CHUNK = BLOCKS * FRAMES
LENGTH = Z * CHUNK
UTTS = 12
ROWS = 32
COLS = 256
HALF = Y * COLS
TILES = HALF // HD
PASSED = TILES + 3
ALL = ("y", "h", "z", "x", "c")
ACROSS = ("y", "h", "z")
BF = jnp.bfloat16
F32 = jnp.float32

VMEM = pl.BlockSpec(memory_space=pltpu.VMEM)
SMEM = pl.BlockSpec(memory_space=pltpu.SMEM)


def call(kernel, outs, *args, scratch=(), smem=0, where=pltpu.VMEM, after=(), mib=40):
    count = len(args)

    def run(*refs):
        kernel(*refs[:count], *refs[count + len(after) :])

    specs = [SMEM] * smem + [pl.BlockSpec(memory_space=where)] * (count - smem)
    return pl.pallas_call(
        run,
        out_shape=[jax.ShapeDtypeStruct(shape, dtype) for shape, dtype in outs],
        in_specs=specs + [pl.BlockSpec(memory_space=pl.ANY)] * len(after),
        out_specs=[VMEM] * len(outs),
        scratch_shapes=list(scratch),
        compiler_params=pltpu.CompilerParams(vmem_limit_bytes=mib * 1024 * 1024),
    )(*args, *after)


def gate(value, after):
    anywhere = pl.BlockSpec(memory_space=pl.ANY)
    return pl.pallas_call(
        lambda *refs: None,
        out_shape=jax.ShapeDtypeStruct(value.shape, value.dtype),
        in_specs=[anywhere] * (1 + len(after)),
        out_specs=anywhere,
        input_output_aliases={0: 0},
    )(value, *after)


def dot(a, b, left=1, right=0):
    return lax.dot_general(
        a, b, (((left,), (right,)), ((), ())), preferred_element_type=F32
    )


def limits(off_ref, u, plane):
    base = plane * CHUNK
    end = off_ref[0, u + 1] if u + 1 < UTTS else LENGTH
    return off_ref[0, u] - base, end - base


def present(off_ref, u, plane):
    low, high = limits(off_ref, u, plane)
    return (low < CHUNK) & (high > 0)


def row_mask(off_ref, u, plane):
    low, high = limits(off_ref, u, plane)
    rows = lax.broadcasted_iota(jnp.int32, (CHUNK, HD), 0)
    return (rows >= low) & (rows < high)


def lane_mask(off_ref, u, plane):
    low, high = limits(off_ref, u, plane)
    lanes = lax.broadcasted_iota(jnp.int32, (HD, CHUNK), 1)
    return (lanes >= low) & (lanes < high)


def scale_of(off_ref, u, plane):
    low, high = limits(off_ref, u, plane)
    span = jnp.full((1, HD), HD * (high - low), jnp.int32).astype(F32)
    return 1.0 / jnp.sqrt(span)


def utterance_at(off_ref, frame):
    count = jnp.int32(-1)
    for u in range(UTTS):
        count = count + (off_ref[0, u] <= frame).astype(jnp.int32)
    return count


def partial_sums(off_ref, plane, left_t, right, own_ref):
    for u in range(UTTS):

        @pl.when(present(off_ref, u, plane))
        def _(u=u):
            masked = jnp.where(lane_mask(off_ref, u, plane), left_t, 0.0).astype(BF)
            own_ref[u] = dot(masked, right)

    first = utterance_at(off_ref, plane * CHUNK)
    last = utterance_at(off_ref, plane * CHUNK + CHUNK - 1)
    return [
        own_ref[jnp.where(plane + shift < Z, last, first)].astype(BF) for shift in range(1, Z)
    ]


def edge_utterances(off_ref, plane):
    found = []
    for shift in range(1, Z):
        source = lax.rem(plane + Z - shift, Z)
        frame = source * CHUNK + jnp.where(source < plane, CHUNK - 1, 0)
        found.append(utterance_at(off_ref, frame))
    return found


def whole_sum(u, own_ref, edge_refs, which, found):
    total = own_ref[u]
    for edge_ref, utterance in zip(edge_refs, found):
        total = total + edge_ref[which].astype(F32) * (utterance == u).astype(F32)
    return total.astype(BF)


def prepare_kernel(q_ref, k_ref, v_ref, cot_ref, keep_ref, give_ref, sems):
    core = lax.axis_index("c")
    copies = []
    for side, (ref, whose) in enumerate(((give_ref, 1 - core), (keep_ref, core))):
        for pair in range(X):
            start = pl.multiple_of((pair * C + whose) * HD, HD)
            for place, source in enumerate((q_ref, k_ref, v_ref)):
                copies.append((source.at[0, :, pl.ds(start, HD)], ref.at[pair * 3 + place], side))
        for tile in range(TILES):
            start = (tile // 2) * C * COLS + whose * COLS + (tile % 2) * HD
            start = pl.multiple_of(start, HD)
            copies.append((cot_ref.at[0, :, pl.ds(start, HD)], ref.at[X * 3 + tile], side))
    copies = [
        pltpu.make_async_copy(source, target, sems.at[i])
        for i, (source, target, _) in enumerate(copies)
    ]
    for copy in copies:
        copy.start()
    for copy in copies:
        copy.wait()


def merge_kernel(keep_ref, came_ref, self_ref, next_ref, back_ref):
    core = lax.axis_index("c")
    x = lax.axis_index("x")
    far = lax.rem(x + 2, X) * 3
    for mine, block in ((keep_ref, core), (came_ref, 1 - core)):
        for first, out, shift in ((0, next_ref, 1), (1, back_ref, 3)):
            near = lax.rem(x + shift, X) * 3
            cot = jnp.where(block == first, 0, PASSED)
            out[pl.ds(cot, TILES)] = mine[X * 3 :]
            out[pl.ds(PASSED + TILES + block * 3, 3)] = mine[pl.ds(near, 3)]

            @pl.when(block == first)
            def _(mine=mine, out=out):
                out[TILES:PASSED] = mine[pl.ds(far, 3)]

        self_ref[pl.ds(block * TILES, TILES)] = mine[X * 3 :]
        self_ref[pl.ds(C * TILES + block * 3, 3)] = mine[pl.ds(x * 3, 3)]


def sources():
    x = lax.axis_index("x")
    return (x, lax.rem(x + X - 1, X), lax.rem(x + 1, X), lax.rem(x + 2, X))


def state_kernel(off_ref, s0, s1, s2, far0, far1, heads_ref, own_ref, edge_ref):
    plane = lax.axis_index("z")
    parts = [[ref[start : start + 3] for start in starts] for ref, starts in (
        (s0, (C * TILES, C * TILES + 3)),
        (s1, (PASSED + TILES, PASSED + TILES + 3)),
        (s2, (PASSED + TILES, PASSED + TILES + 3)),
    )]
    parts.append([far0[TILES:], far1[TILES:]])
    for pair, source in zip(parts, sources()):
        for core, part in enumerate(pair):
            heads_ref[source * C + core] = part
    key = heads_ref[:, 1].reshape(CHUNK, HD).astype(F32)
    value = heads_ref[:, 2].reshape(CHUNK, HD)
    edges = partial_sums(off_ref, plane, key.T, value, own_ref)
    for place, edge in enumerate(edges):
        edge_ref[place] = edge


def attended_kernel(off_ref, heads_ref, own_ref, e1, e2, e3, attended_ref, state_ref, total_ref):
    plane = lax.axis_index("z")
    found = edge_utterances(off_ref, plane)
    query = heads_ref[:, 0].reshape(CHUNK, HD)
    for u in range(UTTS):

        @pl.when(present(off_ref, u, plane))
        def _(u=u):
            state = whole_sum(u, own_ref, (e1, e2, e3), 0, found)
            state_ref[u] = state
            rows = dot(query, state) * scale_of(off_ref, u, plane)
            total_ref[...] = jnp.where(row_mask(off_ref, u, plane), rows, total_ref[...])

    attended_ref[...] = total_ref[...].astype(BF).reshape(BLOCKS, FRAMES, HD)


def wide(tiles):
    return jnp.concatenate([tiles[i] for i in range(TILES)], axis=1)


def chip_cotangents(s0, s1, s2, far0, far1):
    parts = (
        (s0[:TILES], s0[TILES : 2 * TILES]),
        (s1[:TILES], s1[PASSED : PASSED + TILES]),
        (s2[PASSED : PASSED + TILES], s2[:TILES]),
        (far0[:TILES], far1[:TILES]),
    )
    for pair, source in zip(parts, sources()):
        yield source, jnp.concatenate([wide(part) for part in pair], axis=0)


def cotangent_kernel(pieces_ref, s0, s1, s2, far0, far1, mine_ref, theirs_ref, weight_ref):
    core = lax.axis_index("c")
    for y in range(Y):
        for h in range(H):
            for z in range(Z):
                row = (z * H + h) * ROWS
                weight_ref[row : row + ROWS, y * COLS : (y + 1) * COLS] = pieces_ref[
                    (y * H + h) * Z + z
                ]
    weight = weight_ref[...]
    for source, rows in chip_cotangents(s0, s1, s2, far0, far1):
        back = dot(rows, weight, 1, 1)
        low, high = back[:, :HD], back[:, HD:]
        mine = jnp.where(core == 0, low, high)
        theirs = jnp.where(core == 0, high, low)
        for c in range(C):
            mine_ref[source * C + c] = mine[c * FRAMES : (c + 1) * FRAMES]
            theirs_ref[source * C + c] = theirs[c * FRAMES : (c + 1) * FRAMES]


def gradient_kernel(
    off_ref, heads_ref, mine_ref, came_ref, edge_ref, scaled_ref, own_ref, o1, o2, o3, total_ref
):
    plane = lax.axis_index("z")
    back = (mine_ref[...] + came_ref[...]).reshape(CHUNK, HD)
    for u in range(UTTS):

        @pl.when(present(off_ref, u, plane))
        def _(u=u):
            rows = back * scale_of(off_ref, u, plane)
            total_ref[...] = jnp.where(row_mask(off_ref, u, plane), rows, total_ref[...])

    scaled = total_ref[...].astype(BF)
    scaled_ref[...] = scaled
    query = heads_ref[:, 0].reshape(CHUNK, HD).astype(F32)
    edges = partial_sums(off_ref, plane, query.T, scaled, own_ref)
    for place, (edge, out) in enumerate(zip(edges, (o1, o2, o3))):
        out[0] = edge_ref[place]
        out[1] = edge


def weight_kernel(own_ref, partner_ref, s0, s1, s2, far0, far1, term_ref, pair_ref):
    core = lax.axis_index("c")
    own, partner = own_ref[...], partner_ref[...]
    pair_ref[:, 0] = jnp.where(core == 0, own, partner)
    pair_ref[:, 1] = jnp.where(core == 0, partner, own)
    term = None
    for source, right in chip_cotangents(s0, s1, s2, far0, far1):
        left = jnp.concatenate(
            [
                jnp.concatenate([pair_ref[source * C + c, head] for head in range(C)], axis=1)
                for c in range(C)
            ],
            axis=0,
        )
        part = dot(left, right, 0, 0)
        term = part if term is None else term + part
    term = term.astype(BF)
    for y in range(Y):
        for h in range(H):
            for z in range(Z):
                row = (z * H + h) * ROWS
                term_ref[(y * H + h) * Z + z] = term[
                    row : row + ROWS, y * COLS : (y + 1) * COLS
                ]


def home_kernel(
    off_ref, heads_ref, scaled_ref, state_ref, att_ref, partner_ref, own_ref, e1, e2, e3, *refs
):
    outs, (gq, gk, gv) = refs[:X], refs[X:]
    plane = lax.axis_index("z")
    x = lax.axis_index("x")
    core = lax.axis_index("c")
    found = edge_utterances(off_ref, plane)
    key = heads_ref[:, 1].reshape(CHUNK, HD)
    value = heads_ref[:, 2].reshape(CHUNK, HD)
    scaled = scaled_ref[...]
    for u in range(UTTS):

        @pl.when(present(off_ref, u, plane))
        def _(u=u):
            grad = whole_sum(u, own_ref, (e1, e2, e3), 1, found)
            mask = row_mask(off_ref, u, plane)
            gq[...] = jnp.where(mask, dot(scaled, state_ref[u], 1, 1), gq[...])
            gk[...] = jnp.where(mask, dot(value, grad, 1, 1), gk[...])
            gv[...] = jnp.where(mask, dot(key, grad), gv[...])

    for shift, out in enumerate(outs):
        for c in range(C):
            block = lax.rem(x + shift, X) * C + c
            rows = pl.ds(pl.multiple_of(block * FRAMES, FRAMES), FRAMES)
            for place, ref in enumerate((gq, gk, gv)):
                out[c, place] = ref[rows, :].astype(BF)
            out[c, 3 + core] = att_ref[block]
            out[c, 4 - core] = partner_ref[block]


def encode_kernel(r0, r1, r2, r3, w0, w1, w2, top, bottom, keep_ref, give_ref):
    core = lax.axis_index("c")
    total = None
    weights = (w0[...], w1[...], w2[...], jnp.concatenate([top[...], bottom[...]], axis=0))
    for ref, weight, source in zip((r0, r1, r2, r3), weights, sources()):
        for place in range(3):
            keep_ref[source * 3 + place] = ref[core, place]
            give_ref[source * 3 + place] = ref[1 - core, place]
        left = jnp.concatenate(
            [jnp.concatenate([ref[c, 3], ref[c, 4]], axis=1) for c in range(C)], axis=0
        )
        part = dot(left, weight)
        total = part if total is None else total + part
    total = total.astype(BF)
    zero, one = total[:FRAMES], total[FRAMES:]
    mine = jnp.where(core == 0, zero, one)
    theirs = jnp.where(core == 0, one, zero)
    for tile in range(TILES):
        columns = slice(tile * HD, (tile + 1) * HD)
        keep_ref[X * 3 + tile] = mine[:, columns]
        give_ref[X * 3 + tile] = theirs[:, columns]


def finish_kernel(keep_ref, came_ref, enc_ref, q_ref, k_ref, v_ref):
    core = lax.axis_index("c")

    def place_all(parts):
        for c, part in enumerate(parts):
            for pair in range(X):
                start = (pair * C + c) * HD
                for place, ref in enumerate((q_ref, k_ref, v_ref)):
                    ref[0, :, start : start + HD] = part[pair * 3 + place]
            for tile in range(TILES):
                start = (tile // 2) * C * COLS + c * COLS + (tile % 2) * HD
                enc_ref[0, :, start : start + HD] = part[X * 3 + tile]

    @pl.when(core == 0)
    def _():
        place_all((keep_ref, came_ref))

    @pl.when(core == 1)
    def _():
        place_all((came_ref, keep_ref))


def flat(y, h, z, x, c):
    return (((y * H + h) * Z + z) * X + x) * C + c


def swap_pairs():
    return [
        (flat(y, h, z, x, c), flat(y, c, x, z, h))
        for y in range(Y)
        for h in range(H)
        for z in range(Z)
        for x in range(X)
        for c in range(C)
    ]


def turn(value, axis, size, shift):
    return lax.ppermute(value, axis, [(i, (i + shift) % size) for i in range(size)])


def swap_cores(value):
    return turn(value, "c", C, 1)


def body(queries, key_vectors, values, cotangent, out_weight, offsets):
    group = Y * H * Z
    state_shape = (UTTS, HD, HD)
    edge_shape = (2, HD, HD)
    side = (X * 3 + TILES, FRAMES, HD)
    chunk_scratch = pltpu.VMEM((CHUNK, HD), F32)

    moved = lax.ppermute(out_weight, ALL, swap_pairs())
    pieces = lax.all_to_all(
        jnp.broadcast_to(moved[None], (group, ROWS, COLS)), ACROSS, 0, 0, tiled=True
    )
    keep, give = call(
        prepare_kernel,
        [(side, BF)] * 2,
        queries,
        key_vectors,
        values,
        cotangent,
        scratch=[pltpu.SemaphoreType.DMA((2 * side[0],))],
        where=pl.ANY,
        mib=60,
    )
    s0, to_next, to_back = call(
        merge_kernel,
        [((C * PASSED, FRAMES, HD), BF)] + [((C * PASSED + 3, FRAMES, HD), BF)] * 2,
        keep,
        swap_cores(give),
    )
    s1, s2 = turn(to_next, "x", X, 1), turn(to_back, "x", X, -1)
    rows = (s0, s1, s2, turn(s1[:PASSED], "x", X, 1), turn(s2[:PASSED], "x", X, -1))

    mine, theirs, weight = call(
        cotangent_kernel,
        [((BLOCKS, FRAMES, HD), F32)] * 2 + [((2 * HD, HALF), BF)],
        pieces,
        *rows,
    )
    w1, w2 = turn(weight, "x", X, 1), turn(weight, "x", X, -1)
    top, bottom = turn(w1[:HD], "x", X, 1), turn(w2[HD:], "x", X, -1)
    heads, own, edge = call(
        state_kernel,
        [((BLOCKS, 3, FRAMES, HD), BF), (state_shape, F32), ((Z - 1, HD, HD), BF)],
        offsets,
        *rows,
        smem=1,
        after=[theirs],
    )
    scaled, gown, *edges = call(
        gradient_kernel,
        [((CHUNK, HD), BF), (state_shape, F32)] + [(edge_shape, BF)] * (Z - 1),
        offsets,
        heads,
        mine,
        swap_cores(theirs),
        edge,
        scratch=[chunk_scratch],
        smem=1,
    )
    edges = [turn(part, "z", Z, shift) for shift, part in enumerate(edges, 1)]
    attended, state = call(
        attended_kernel,
        [((BLOCKS, FRAMES, HD), BF), (state_shape, BF)],
        offsets,
        heads,
        own,
        *edges,
        scratch=[chunk_scratch],
        smem=1,
        after=[w1, w2],
    )
    partner = swap_cores(attended)
    r0, h1, h2, h3 = call(
        home_kernel,
        [((C, 5, FRAMES, HD), BF)] * X,
        offsets,
        heads,
        scaled,
        state,
        attended,
        partner,
        gown,
        *edges,
        scratch=[chunk_scratch] * 3,
        smem=1,
    )
    (term,) = call(
        weight_kernel,
        [((group, ROWS, COLS), BF)],
        attended,
        partner,
        *rows,
        scratch=[pltpu.VMEM((BLOCKS, C, FRAMES, HD), BF)],
    )
    h1, h2, h3 = turn(h1, "x", X, 1), turn(h2, "x", X, 2), turn(h3, "x", X, -1)
    term = lax.all_to_all(gate(term, [r0, top, bottom]), ACROSS, 0, 0, tiled=True)
    grad_weight = jnp.sum(term.astype(F32), axis=0) / math.sqrt(Y * H * LENGTH)
    grad_weight = lax.ppermute(grad_weight, ALL, swap_pairs())

    keep, give = call(
        encode_kernel,
        [(side, BF)] * 2,
        r0,
        h1,
        h3,
        h2,
        weight,
        w1,
        w2,
        top,
        bottom,
    )
    encoded, *grads = call(
        finish_kernel,
        [((1, FRAMES, C * HALF), BF)] + [((1, FRAMES, BLOCKS * HD), BF)] * 3,
        keep,
        swap_cores(give),
    )
    return (encoded, grads[0], grads[1], grads[2], grad_weight)


def solution(mesh):
    fine = Mesh(np.asarray(mesh.devices).reshape(Y, H, Z, X, C), ALL)
    dp, tm = ("y", "h"), ("z", "x", "c")
    three = P(dp, tm, None)
    in_specs = (three, three, three, three, P(tm, dp), P(dp, None))
    out_specs = (three, three, three, three, P(tm, dp))
    return jax.shard_map(body, mesh=fine, in_specs=in_specs, out_specs=out_specs, check_vma=False)
```
